256 devices in a mesh: freq: 4 (over y_hi, core), space: 64 (over x, y_lo, z).
Axes of the slice: x: 4, y: 4 (y_hi: 2, y_lo: 2; y = y_hi * 2 + y_lo), z: 8, core: 2. Of those that a mesh axis runs over, the one named last changes fastest.
Arguments:
- reflection: float32 [2, 32, 1024, 1024], P(None, 'freq', 'space'), may hold values from -6 to 6
- phase: float32 [32, 1024], P('freq'), may hold values from -3.140625 to 3.140625
- group_index: int32 [32], P('freq'), may hold values from 0 to 3
- widths: int32 [64, 2], P('space'), may hold values from 1 to 16
Outputs:
- corrected: float32 [2, 4, 1024, 1024], P(None, 'freq', None, 'space')
The draws below stay inside these ranges and needn't reach their ends.
Inputs may be any that keep to these rules, and one draw needn't show every extreme that they name: `group_index`: each frequency belongs to one depth group. `widths`: margins of a patch are at most one column block wide.
All inputs are finite; a program needn't handle non-finite values.
Results may differ from the reference program's by a relative error of at most 0.0003.
Values sent between devices are 32-bit elements; how exact they have to be, the bound alone decides.
A program may use at most 64 MiB of HBM per device.

```python
import jax
import jax.numpy as jnp
from jax import lax

N = 1024
ITERS = 3
NF = 32
GROUPS = 4
CB = 16
PATCHES = 64
N_SPACE = 64


def set_ends(result, rng, low, top_value):
    longest = result.shape.index(max(result.shape))
    spots = []
    for shift in (0, 1):
        where = [jax.random.randint(jax.random.fold_in(rng, axis), (), 0, length) for axis, length in enumerate(result.shape)]
        where[longest] = (where[longest] + shift) % result.shape[longest]
        spots.append(tuple(where))
    return result.at[spots[0]].set(low).at[spots[1]].set(top_value)


def block_levels(own_key, extent, cuts, low, largest):
    def one(axis_at, shards_of):
        draws = jax.random.uniform(jax.random.fold_in(jax.random.fold_in(own_key, 6), axis_at), (shards_of,), jnp.float32, low / len(cuts), largest / len(cuts))
        return jnp.repeat(jnp.exp(draws), extent[axis_at] // shards_of).reshape((-1,) + (1,) * (len(extent) - axis_at - 1))

    level = one(*cuts[0])
    for cut in cuts[1:]:
        level = level * one(*cut)
    return level


def bell_draw(stream_key, shape, spread, reach, pieces=(), kind=jnp.bfloat16):
    drawn = jax.random.normal(stream_key, shape, jnp.float32) * spread
    if len(pieces) > 0:
        drawn = block_levels(stream_key, shape, pieces, -0.22, 0.18) * drawn
    return jnp.clip(drawn, min=-reach, max=reach).astype(kind)


def setup_inputs(seed: int = 0) -> dict:
    key_list = jax.random.split(jax.random.key(seed), 5)
    return {
        "reflection": bell_draw(key_list[0], (2, NF, N, N), 1.0, 6.0, ((1, 4), (2, 64)), jnp.float32),
        "phase": jnp.clip(jax.random.uniform(key_list[1], (NF, N), jnp.float32, -3.140625, 3.140625), -3.140625, 3.140625),
        "group_index": set_ends(jax.random.randint(key_list[2], (NF,), 0, GROUPS), jax.random.fold_in(key_list[2], 1), 0, GROUPS - 1).astype(jnp.int32),
        "widths": set_ends(jax.random.randint(key_list[3], (PATCHES, 2), 1, CB + 1), jax.random.fold_in(key_list[3], 1), 1, CB).astype(jnp.int32),
    }


def normalize(real_part, imag_part):
    power = real_part * real_part + imag_part * imag_part
    scale = 1.0 / jnp.sqrt(power + lax.optimization_barrier(jnp.mean(power, axis=0, keepdims=True)) + 1e-06)
    return (real_part * scale, imag_part * scale)

def reference(reflection, phase, group_index, widths):
    width = reflection.shape[2]
    block = width // N_SPACE
    group_ids = jnp.arange(GROUPS, dtype=jnp.int32)

    def add_one(total, index):
        plane_r = lax.dynamic_index_in_dim(reflection[0], index, 0, keepdims=False)
        plane_i = lax.dynamic_index_in_dim(reflection[1], index, 0, keepdims=False)
        angle = lax.dynamic_index_in_dim(phase, index, 0, keepdims=False)
        cosine = jnp.cos(angle)[None, :]
        sine = jnp.sin(angle)[None, :]
        turned = jnp.stack([plane_r * cosine - plane_i * sine, plane_r * sine + plane_i * cosine])
        label = lax.dynamic_index_in_dim(group_index, index, 0, keepdims=False)
        onehot = (group_ids == label).astype(jnp.float32)
        return (total + onehot[:, None, None, None] * turned[None], None)
    start = jnp.zeros((GROUPS, 2, width, width), jnp.float32)
    focused, _ = lax.scan(add_one, start, jnp.arange(NF, dtype=jnp.int32))
    position = jnp.arange(block, dtype=jnp.int32)
    left_keep = (position[None, :] >= block - widths[:, 0:1]).astype(jnp.float32)
    right_keep = (position[None, :] < widths[:, 1:2]).astype(jnp.float32)
    root = jnp.sqrt(jnp.float32(width))
    results = []
    for group in range(GROUPS):
        field = focused[group, 0] + 1j * focused[group, 1]
        spectrum = jnp.fft.fft(jnp.fft.fft(field, axis=1) / root, axis=0) / root
        whole_r = jnp.real(spectrum).astype(jnp.float32).reshape(width, N_SPACE, block)
        whole_i = jnp.imag(spectrum).astype(jnp.float32).reshape(width, N_SPACE, block)
        patch_r = jnp.concatenate([jnp.roll(whole_r, 1, axis=1) * left_keep, whole_r, jnp.roll(whole_r, -1, axis=1) * right_keep], axis=2)
        patch_i = jnp.concatenate([jnp.roll(whole_i, 1, axis=1) * left_keep, whole_i, jnp.roll(whole_i, -1, axis=1) * right_keep], axis=2)
        vector_r, vector_i = normalize(lax.optimization_barrier(jnp.sum(patch_r, axis=2)), lax.optimization_barrier(jnp.sum(patch_i, axis=2)))
        for step in range(ITERS):
            back_r = jnp.einsum('rjc,rj->jc', patch_r, vector_r, precision=lax.Precision.HIGHEST) + jnp.einsum('rjc,rj->jc', patch_i, vector_i, precision=lax.Precision.HIGHEST)
            back_i = jnp.einsum('rjc,rj->jc', patch_r, vector_i, precision=lax.Precision.HIGHEST) - jnp.einsum('rjc,rj->jc', patch_i, vector_r, precision=lax.Precision.HIGHEST)
            next_r = jnp.einsum('rjc,jc->rj', patch_r, back_r, precision=lax.Precision.HIGHEST) - jnp.einsum('rjc,jc->rj', patch_i, back_i, precision=lax.Precision.HIGHEST)
            next_i = jnp.einsum('rjc,jc->rj', patch_r, back_i, precision=lax.Precision.HIGHEST) + jnp.einsum('rjc,jc->rj', patch_i, back_r, precision=lax.Precision.HIGHEST)
            vector_r, vector_i = normalize(next_r, next_i)
        fixed_r = vector_r[:, :, None] * whole_r + vector_i[:, :, None] * whole_i
        fixed_i = vector_r[:, :, None] * whole_i - vector_i[:, :, None] * whole_r
        results.append(jnp.stack([fixed_r.reshape(width, width), fixed_i.reshape(width, width)]))
    return jnp.stack(results, axis=1)
```

```python
import functools
import math

import jax
import jax.numpy as jnp
import ml_dtypes
import numpy as np
from jax import lax
from jax.experimental import pallas as pl
from jax.experimental.pallas import tpu as pltpu
from jax.sharding import PartitionSpec as P

MESH = pl.DeviceIdType.MESH
F32 = jnp.float32
BF16 = jnp.bfloat16
ITERS = 3
N = 1024
NFD = 8
ROWS = 16
EPS = 1e-06


def split_np(table):
    hi = table.astype(np.float32).astype(ml_dtypes.bfloat16)
    lo = (table - hi.astype(np.float64)).astype(np.float32).astype(ml_dtypes.bfloat16)
    return np.stack([hi, lo])


def tables():
    lane = np.arange(128)
    k1 = np.arange(8)
    ang = 2 * np.pi * (k1[:, None] * lane[None, :] % N) / N
    twist_a = np.stack([np.cos(ang), np.sin(ang)]) / 32.0
    y_lo, x, slot, q_hi = np.meshgrid(np.arange(2), np.arange(4), np.arange(10), np.arange(2), indexing="ij")
    block = ((x * 2 + y_lo) * 8 + slot - 1) % 64
    k2 = (2 * block + q_hi).reshape(-1)
    ang = 2 * np.pi * (k2[:, None] * lane[None, :] % 128) / 128
    cos, sin = (np.cos(ang), np.sin(ang))
    real_rows = np.concatenate([cos, sin], axis=1)
    imag_rows = np.concatenate([-sin, cos], axis=1)
    col = np.stack([real_rows, imag_rows], axis=1).reshape(320, 256)
    row = np.zeros((2, 2, 2, 64, 4, 8, 2, 2, 2))
    m1 = np.arange(64)
    for mine in range(2):
        for rel in range(2):
            xs, zs = np.meshgrid(np.arange(4), np.arange(8), indexing="ij")
            s = (xs * 2 + (mine ^ rel)) * 8 + zs
            ang = 2 * np.pi * (m1[:, None, None] * s[None] % 64) / 64
            for q in range(2):
                row[mine, 0, q, :, :, :, rel, q, 0] = np.cos(ang)
                row[mine, 0, q, :, :, :, rel, q, 1] = np.sin(ang)
                row[mine, 1, q, :, :, :, rel, q, 0] = -np.sin(ang)
                row[mine, 1, q, :, :, :, rel, q, 1] = np.cos(ang)
    row = row.reshape(2, 256, 256)
    ang = 2 * np.pi * (m1[:, None] * (lane % 16)[None, :] % N) / N
    twist_b = np.stack([np.cos(ang), np.sin(ang)])
    last = np.zeros((2, 8, 16, 2, 16, 8))
    i, m2 = (np.arange(16), np.arange(16))
    ang = 2 * np.pi * (i[:, None] * m2[None, :] % 16) / 16
    for k in range(8):
        last[0, k, :, 0, :, k] = np.cos(ang)
        last[1, k, :, 0, :, k] = np.sin(ang)
        last[0, k, :, 1, :, k] = -np.sin(ang)
        last[1, k, :, 1, :, k] = np.cos(ang)
    last = last.reshape(256, 256) / 32.0
    over_k1 = (lane[:, None] // 8 == lane[None, :] // 8).astype(np.float64)
    over_m2 = (lane[:, None] % 8 == lane[None, :] % 8).astype(np.float64)
    sums = np.stack([np.concatenate([t, t], axis=0) for t in (over_k1, over_m2)]).astype(ml_dtypes.bfloat16)
    return (
        twist_a.astype(np.float32),
        split_np(col),
        np.moveaxis(split_np(row), 0, 1),
        twist_b.astype(np.float32),
        split_np(last),
        sums,
    )


def halves(value):
    hi = value.astype(BF16)
    lo = (value - hi.astype(F32)).astype(BF16)
    return (hi, lo)


def dft4(v):
    (ar, ai), (br, bi), (cr, ci), (dr, di) = v
    pr, pi, mr, mi = (ar + cr, ai + ci, ar - cr, ai - ci)
    qr, qi, nr, ni = (br + dr, bi + di, br - dr, bi - di)
    return [(pr + qr, pi + qi), (mr + ni, mi - nr), (pr - qr, pi - qi), (mr - ni, mi + nr)]


def dft8(v):
    even = dft4(v[0::2])
    odd = dft4(v[1::2])
    half = math.sqrt(0.5)
    o1r, o1i = odd[1]
    o2r, o2i = odd[2]
    o3r, o3i = odd[3]
    turned = [
        odd[0],
        ((o1r + o1i) * half, (o1i - o1r) * half),
        (o2i, -o2r),
        ((o3i - o3r) * half, -(o3r + o3i) * half),
    ]
    low = [(e[0] + t[0], e[1] + t[1]) for e, t in zip(even, turned)]
    high = [(e[0] - t[0], e[1] - t[1]) for e, t in zip(even, turned)]
    return low + high


def matmul(left, right):
    return jnp.dot(left, right, preferred_element_type=F32)


def matmul_t(left, right):
    return lax.dot_general(left, right, (((1,), (1,)), ((), ())), preferred_element_type=F32)


def wait_bytes(ref, sem):
    pltpu.make_async_copy(ref, ref, sem).wait()


def kernel(
    refl_hbm, phase_hbm, group_hbm, widths_hbm, twa_hbm, col_hbm, row_hbm, twb_hbm, last_hbm, sums_hbm,
    out_ref,
    refl, phase, group, widths, twa, col, row, twb, last, sums,
    core_out, core_own, core_in, xsplit, y_out, y_in, q_buf, r_buf, rsplit, vsplit, t_buf,
    load_sem, core_sem, y_sem, a2a_sem,
):
    f = lax.axis_index("freq")
    s = lax.axis_index("space")
    y_hi = f // 2
    core = lax.rem(f, 2)
    x = s // 16
    y_lo = lax.rem(s // 8, 2)
    z = lax.rem(s, 8)

    loads = [
        pltpu.make_async_copy(src, dst, load_sem.at[n])
        for n, (src, dst) in enumerate(
            [
                (group_hbm, group), (phase_hbm, phase), (refl_hbm, refl), (twa_hbm, twa), (col_hbm, col),
                (row_hbm.at[y_lo], row), (twb_hbm, twb), (last_hbm, last), (sums_hbm, sums), (widths_hbm, widths),
            ]
        )
    ]
    for load in loads:
        load.start()

    core_peer = (y_hi * 2 + 1 - core, s)
    other_f = (1 - y_hi) * 2 + core
    other_s = (x * 2 + 1 - y_lo) * 8 + z
    y_peers = [(other_f, s), (f, other_s), (other_f, other_s)]
    steps = sorted(
        [(dx, dz) for dx in range(4) for dz in range(8) if dx or dz],
        key=lambda t: -(min(t[0], 4 - t[0]) + min(t[1], 8 - t[1])),
    )
    places = [(lax.rem(x + dx, 4), lax.rem(z + dz, 8)) for dx, dz in steps]
    a2a_peers = [(f, (px * 2 + y_lo) * 8 + pz) for px, pz in places]

    barrier = pltpu.get_barrier_semaphore()
    everyone = a2a_peers + y_peers + [core_peer]
    for peer in everyone:
        pl.semaphore_signal(barrier, inc=1, device_id=peer, device_id_type=MESH)

    loads[0].wait()
    loads[1].wait()
    angle = phase[...]
    cosine = jnp.cos(angle)
    sine = jnp.sin(angle)
    weights = [
        [(group[k] == 2 * gh + gc).astype(F32) for gh in range(2) for gc in (1 - core, core)] for k in range(NFD)
    ]
    loads[2].wait()
    for a in range(8):
        lanes = slice(128 * a, 128 * a + 128)
        total = [[None, None] for _ in range(4)]
        for k in range(NFD):
            c = cosine[k : k + 1, lanes]
            d = sine[k : k + 1, lanes]
            re = refl[0, k, :, lanes]
            im = refl[1, k, :, lanes]
            turned = (re * c - im * d, re * d + im * c)
            for g in range(4):
                for part in range(2):
                    term = turned[part] * weights[k][g]
                    total[g][part] = term if k == 0 else total[g][part] + term
        for gh in range(2):
            for part in range(2):
                core_out[gh, part, :, lanes] = total[2 * gh][part]
                core_own[gh, part, :, lanes] = total[2 * gh + 1][part]

    pl.semaphore_wait(barrier, len(everyone))
    core_copy = pltpu.make_async_remote_copy(
        src_ref=core_out, dst_ref=core_in, send_sem=core_sem.at[0], recv_sem=core_sem.at[1],
        device_id=core_peer, device_id_type=MESH,
    )
    core_copy.start()
    loads[3].wait()
    loads[4].wait()
    core_copy.wait_recv()

    for gh in range(2):
        tiles = []
        for a in range(8):
            lanes = slice(128 * a, 128 * a + 128)
            tiles.append(tuple(core_own[gh, part, :, lanes] + core_in[gh, part, :, lanes] for part in range(2)))
        mixed = dft8(tiles)
        for k in range(8):
            vr, vi = mixed[k]
            c = twa[0, k : k + 1, :]
            d = twa[1, k : k + 1, :]
            first = gh * 128 + k * ROWS
            for part, value in enumerate((vr * c + vi * d, vi * c - vr * d)):
                hi, lo = halves(value)
                xsplit[0, first : first + ROWS, part * 128 : part * 128 + 128] = hi
                xsplit[1, first : first + ROWS, part * 128 : part * 128 + 128] = lo
    y = matmul_t(col[0], xsplit[0]) + (matmul_t(col[1], xsplit[0]) + matmul_t(col[0], xsplit[1]))
    for gh in range(2):
        for lo_index in range(2):
            y_out[gh, lo_index] = y[160 * lo_index : 160 * lo_index + 160, 128 * gh : 128 * gh + 128]

    y_copies = []
    for n, (gh, lo_index) in enumerate([(1 - y_hi, y_lo), (y_hi, 1 - y_lo), (1 - y_hi, 1 - y_lo)]):
        copy = pltpu.make_async_remote_copy(
            src_ref=y_out.at[gh, lo_index], dst_ref=y_in.at[n], send_sem=y_sem.at[0, n], recv_sem=y_sem.at[1, n],
            device_id=y_peers[n], device_id_type=MESH,
        )
        copy.start()
        y_copies.append(copy)
    for copy in y_copies:
        copy.wait_recv()
    low = lax.broadcasted_iota(jnp.int32, (8, 128), 0) < 4
    for t in range(20):
        rows = slice(8 * t, 8 * t + 8)
        near = y_out[y_hi, y_lo, rows, :] + y_in[0, rows, :]
        far = y_in[1, rows, :] + y_in[2, rows, :]
        b = 2 * t
        q_buf[b // 10, b % 10] = jnp.where(low, near, pltpu.roll(far, 4, 0))
        q_buf[b // 10, b % 10 + 1] = jnp.where(low, pltpu.roll(near, 4, 0), far)

    own = x * 8 + z
    for n, (px, pz) in enumerate(places):
        pltpu.make_async_remote_copy(
            src_ref=q_buf.at[px, pl.ds(pz, 3)], dst_ref=r_buf.at[:, own], send_sem=a2a_sem.at[0],
            recv_sem=a2a_sem.at[1], device_id=a2a_peers[n], device_id_type=MESH,
        ).start()
    for b in range(3):
        r_buf[b, own] = q_buf[x, z + b]
    for load in loads[5:]:
        load.wait()
    w_left = widths[0, 0]
    w_right = widths[0, 1]
    wait_bytes(r_buf.at[:, pl.ds(0, 31)], a2a_sem.at[1])

    for b in range(3):
        hi, lo = halves(r_buf[b].reshape(256, 128))
        rsplit[0, :, 128 * b : 128 * b + 128] = hi
        rsplit[1, :, 128 * b : 128 * b + 128] = lo
    mid = matmul(row[0], rsplit[0]) + (matmul(row[1], rsplit[0]) + matmul(row[0], rsplit[1]))
    for b in range(3):
        for q in range(2):
            vr = mid[64 * q : 64 * q + 64, 128 * b : 128 * b + 128]
            vi = mid[128 + 64 * q : 192 + 64 * q, 128 * b : 128 * b + 128]
            first = (b * 2 + q) * 64
            for part, value in enumerate((vr * twb[0] + vi * twb[1], vi * twb[0] - vr * twb[1])):
                hi, lo = halves(value)
                vsplit[0, first : first + 64, 128 * part : 128 * part + 128] = hi
                vsplit[1, first : first + 64, 128 * part : 128 * part + 128] = lo
    t_buf[...] = matmul(vsplit[0], last[0]) + (matmul(vsplit[1], last[0]) + matmul(vsplit[0], last[1]))

    k_lane = lax.rem(lax.broadcasted_iota(jnp.int32, (1, 128), 1), 8)
    keep = []
    for b in range(3):
        for q in range(2):
            column = k_lane + 8 * q
            if b == 0:
                keep.append((column >= 16 - w_left).astype(F32))
            elif b == 1:
                keep.append(jnp.ones((1, 128), F32))
            else:
                keep.append((column < w_right).astype(F32))

    def block(n):
        return (t_buf[64 * n : 64 * n + 64, 0:128], t_buf[64 * n : 64 * n + 64, 128:256])

    def group_sum(value, which):
        hi, lo = halves(value)
        return matmul(jnp.concatenate([hi, lo], axis=1), sums[which])

    def normalized(nr, ni):
        both = group_sum(jnp.concatenate([nr, ni], axis=0), 0)
        vr = both[0:64]
        vi = both[64:128]
        power = vr * vr + vi * vi
        mean = jnp.sum(jnp.sum(power, axis=0, keepdims=True), axis=1, keepdims=True) * (1.0 / (8 * N))
        scale = 1.0 / jnp.sqrt(power + mean + EPS)
        return (vr * scale, vi * scale)

    nr = jnp.zeros((64, 128), F32)
    ni = jnp.zeros((64, 128), F32)
    for n in range(6):
        tr, ti = block(n)
        nr = nr + tr * keep[n]
        ni = ni + ti * keep[n]
    ur, ui = normalized(nr, ni)
    for _ in range(ITERS):
        rows = []
        for n in range(6):
            tr, ti = block(n)
            rows.append(jnp.sum(ur * tr + ui * ti, axis=0, keepdims=True) * keep[n])
            rows.append(jnp.sum(ui * tr - ur * ti, axis=0, keepdims=True) * keep[n])
        rows.append(jnp.zeros((4, 128), F32))
        back = group_sum(jnp.concatenate(rows, axis=0), 1)
        nr = jnp.zeros((64, 128), F32)
        ni = jnp.zeros((64, 128), F32)
        for n in range(6):
            tr, ti = block(n)
            br = back[2 * n : 2 * n + 1, :]
            bi = back[2 * n + 1 : 2 * n + 2, :]
            nr = nr + (tr * br - ti * bi)
            ni = ni + (tr * bi + ti * br)
        ur, ui = normalized(nr, ni)

    fixed = [[], []]
    for q in range(2):
        tr, ti = block(2 + q)
        fixed[0].append(ur * tr + ui * ti)
        fixed[1].append(ur * ti - ui * tr)
    left = lax.broadcasted_iota(jnp.int32, (8, 128), 1) < 64
    for part in range(2):
        turned = jnp.concatenate(fixed[part], axis=0).T
        for p in range(8):
            first = turned[16 * p : 16 * p + 8]
            second = turned[16 * p + 8 : 16 * p + 16]
            out_ref[part, 0:8, 128 * p : 128 * p + 128] = jnp.where(left, first, pltpu.roll(second, 64, 1))
            out_ref[part, 8:16, 128 * p : 128 * p + 128] = jnp.where(left, pltpu.roll(first, 64, 1), second)

    core_copy.wait_send()
    for copy in y_copies:
        copy.wait_send()
    wait_bytes(r_buf.at[:, pl.ds(0, 31)], a2a_sem.at[0])


def local(reflection, phase, group_index, widths):
    consts = [jnp.asarray(t) for t in tables()]
    operands = [reflection, phase, group_index, widths] + consts
    in_specs = [pl.BlockSpec(memory_space=pl.ANY)] * len(operands)
    scratch = [
        pltpu.VMEM((2, NFD, ROWS, N), F32),
        pltpu.VMEM((NFD, N), F32),
        pltpu.SMEM((NFD,), jnp.int32),
        pltpu.SMEM((1, 2), jnp.int32),
        pltpu.VMEM((2, 8, 128), F32),
        pltpu.VMEM((2, 320, 256), BF16),
        pltpu.VMEM((2, 256, 256), BF16),
        pltpu.VMEM((2, 64, 128), F32),
        pltpu.VMEM((2, 256, 256), BF16),
        pltpu.VMEM((2, 256, 128), BF16),
        pltpu.VMEM((2, 2, ROWS, N), F32),
        pltpu.VMEM((2, 2, ROWS, N), F32),
        pltpu.VMEM((2, 2, ROWS, N), F32),
        pltpu.VMEM((2, 256, 256), BF16),
        pltpu.VMEM((2, 2, 160, 128), F32),
        pltpu.VMEM((3, 160, 128), F32),
        pltpu.VMEM((4, 10, 8, 128), F32),
        pltpu.VMEM((3, 32, 8, 128), F32),
        pltpu.VMEM((2, 256, 384), BF16),
        pltpu.VMEM((2, 384, 256), BF16),
        pltpu.VMEM((384, 256), F32),
        pltpu.SemaphoreType.DMA((10,)),
        pltpu.SemaphoreType.DMA((2,)),
        pltpu.SemaphoreType.DMA((2, 3)),
        pltpu.SemaphoreType.DMA((2,)),
    ]
    result = pl.pallas_call(
        kernel,
        out_shape=jax.ShapeDtypeStruct((2, ROWS, N), F32),
        in_specs=in_specs,
        out_specs=pl.BlockSpec(memory_space=pltpu.VMEM),
        scratch_shapes=scratch,
        name="focus",
        compiler_params=pltpu.CompilerParams(
            collective_id=0, has_side_effects=True, vmem_limit_bytes=56 * 1024 * 1024
        ),
    )(*operands)
    return jnp.swapaxes(result, 1, 2)[:, None]


def solution(mesh):
    in_specs = (P(None, "freq", "space", None), P("freq", None), P("freq"), P("space", None))
    out_specs = P(None, "freq", None, "space")
    return jax.shard_map(local, mesh=mesh, in_specs=in_specs, out_specs=out_specs, check_vma=False)
```

```python
import functools
import math

import jax
import jax.numpy as jnp
import ml_dtypes
import numpy as np
from jax import lax
from jax.experimental import pallas as pl
from jax.experimental.pallas import tpu as pltpu
from jax.sharding import PartitionSpec as P

MESH = pl.DeviceIdType.MESH
F32 = jnp.float32
BF16 = jnp.bfloat16
ITERS = 3
N = 1024
NFD = 8
ROWS = 16
EPS = 1e-06


def split_np(table):
    hi = table.astype(np.float32).astype(ml_dtypes.bfloat16)
    lo = (table - hi.astype(np.float64)).astype(np.float32).astype(ml_dtypes.bfloat16)
    return np.stack([hi, lo])


def tables():
    lane = np.arange(128)
    k1 = np.arange(8)
    ang = 2 * np.pi * (k1[:, None] * lane[None, :] % N) / N
    twist_a = np.stack([np.cos(ang), np.sin(ang)]) / 32.0
    y_lo, x, slot, q_hi = np.meshgrid(np.arange(2), np.arange(4), np.arange(10), np.arange(2), indexing="ij")
    block = ((x * 2 + y_lo) * 8 + slot - 1) % 64
    k2 = (2 * block + q_hi).reshape(-1)
    ang = 2 * np.pi * (k2[:, None] * lane[None, :] % 128) / 128
    cos, sin = (np.cos(ang), np.sin(ang))
    real_rows = np.concatenate([cos, sin], axis=1)
    imag_rows = np.concatenate([-sin, cos], axis=1)
    col = np.stack([real_rows, imag_rows], axis=1).reshape(320, 256)
    row = np.zeros((2, 2, 2, 64, 4, 8, 2, 2, 2))
    m1 = np.arange(64)
    for mine in range(2):
        for rel in range(2):
            xs, zs = np.meshgrid(np.arange(4), np.arange(8), indexing="ij")
            s = (xs * 2 + (mine ^ rel)) * 8 + zs
            ang = 2 * np.pi * (m1[:, None, None] * s[None] % 64) / 64
            for q in range(2):
                row[mine, 0, q, :, :, :, rel, q, 0] = np.cos(ang)
                row[mine, 0, q, :, :, :, rel, q, 1] = np.sin(ang)
                row[mine, 1, q, :, :, :, rel, q, 0] = -np.sin(ang)
                row[mine, 1, q, :, :, :, rel, q, 1] = np.cos(ang)
    row = row.reshape(2, 256, 256)
    ang = 2 * np.pi * (m1[:, None] * (lane % 16)[None, :] % N) / N
    twist_b = np.stack([np.cos(ang), np.sin(ang)])
    last = np.zeros((2, 8, 16, 2, 16, 8))
    i, m2 = (np.arange(16), np.arange(16))
    ang = 2 * np.pi * (i[:, None] * m2[None, :] % 16) / 16
    for k in range(8):
        last[0, k, :, 0, :, k] = np.cos(ang)
        last[1, k, :, 0, :, k] = np.sin(ang)
        last[0, k, :, 1, :, k] = -np.sin(ang)
        last[1, k, :, 1, :, k] = np.cos(ang)
    last = last.reshape(256, 256) / 32.0
    over_k1 = (lane[:, None] // 8 == lane[None, :] // 8).astype(np.float64)
    over_m2 = (lane[:, None] % 8 == lane[None, :] % 8).astype(np.float64)
    sums = np.stack([np.concatenate([t, t], axis=0) for t in (over_k1, over_m2)]).astype(ml_dtypes.bfloat16)
    return (
        twist_a.astype(np.float32),
        split_np(col),
        np.moveaxis(split_np(row), 0, 1),
        twist_b.astype(np.float32),
        split_np(last),
        sums,
    )


def halves(value):
    hi = value.astype(BF16)
    lo = (value - hi.astype(F32)).astype(BF16)
    return (hi, lo)


def dft4(v):
    (ar, ai), (br, bi), (cr, ci), (dr, di) = v
    pr, pi, mr, mi = (ar + cr, ai + ci, ar - cr, ai - ci)
    qr, qi, nr, ni = (br + dr, bi + di, br - dr, bi - di)
    return [(pr + qr, pi + qi), (mr + ni, mi - nr), (pr - qr, pi - qi), (mr - ni, mi + nr)]


def dft8(v):
    even = dft4(v[0::2])
    odd = dft4(v[1::2])
    half = math.sqrt(0.5)
    o1r, o1i = odd[1]
    o2r, o2i = odd[2]
    o3r, o3i = odd[3]
    turned = [
        odd[0],
        ((o1r + o1i) * half, (o1i - o1r) * half),
        (o2i, -o2r),
        ((o3i - o3r) * half, -(o3r + o3i) * half),
    ]
    low = [(e[0] + t[0], e[1] + t[1]) for e, t in zip(even, turned)]
    high = [(e[0] - t[0], e[1] - t[1]) for e, t in zip(even, turned)]
    return low + high


def matmul(left, right):
    return jnp.dot(left, right, preferred_element_type=F32)


def matmul_t(left, right):
    return lax.dot_general(left, right, (((1,), (1,)), ((), ())), preferred_element_type=F32)


def wait_bytes(ref, sem):
    pltpu.make_async_copy(ref, ref, sem).wait()


def kernel(
    refl_hbm, phase_hbm, group_hbm, twa_hbm, col_hbm,
    r_buf,
    refl, phase, group, twa, col,
    core_out, core_own, core_in, xsplit, y_out, y_in, q_buf,
    load_sem, core_sem, y_sem, a2a_sem, plane_sem,
):
    f = lax.axis_index("freq")
    s = lax.axis_index("space")
    y_hi = f // 2
    core = lax.rem(f, 2)
    x = s // 16
    y_lo = lax.rem(s // 8, 2)
    z = lax.rem(s, 8)

    loads = [
        pltpu.make_async_copy(src, dst, load_sem.at[n])
        for n, (src, dst) in enumerate(
            [
                (group_hbm, group), (phase_hbm, phase), (refl_hbm, refl), (twa_hbm, twa), (col_hbm, col),
            ]
        )
    ]
    for load in loads:
        load.start()

    core_peer = (y_hi * 2 + 1 - core, s)
    other_f = (1 - y_hi) * 2 + core
    other_s = (x * 2 + 1 - y_lo) * 8 + z
    y_peers = [(other_f, s), (f, other_s), (other_f, other_s)]
    dests = sorted(
        [(px, pz) for px in range(4) for pz in range(8)], key=lambda t: (min(t[1], 4), (0, 1, 2, 2)[t[0]], t[1])
    )
    a2a_peers = [(f, (px * 2 + y_lo) * 8 + pz) for px, pz in dests]
    own = x * 8 + z
    is_other = [own != px * 8 + pz for px, pz in dests]

    barrier = pltpu.get_barrier_semaphore()
    z_ring = [(f, (x * 2 + y_lo) * 8 + lax.rem(z + d, 8)) for d in (4, 3, 5, 2, 6, 1, 7)]
    x_ring = [(f, (lax.rem(x + d, 4) * 2 + y_lo) * 8 + z) for d in (2, 1, 3)]
    first_peers = [core_peer] + y_peers + x_ring + z_ring
    for peer in first_peers:
        pl.semaphore_signal(barrier, inc=1, device_id=peer, device_id_type=MESH)

    loads[0].wait()
    loads[1].wait()
    angle = phase[...]
    cosine = jnp.cos(angle)
    sine = jnp.sin(angle)
    weights = [
        [(group[k] == 2 * gh + gc).astype(F32) for gh in range(2) for gc in (1 - core, core)] for k in range(NFD)
    ]
    loads[2].wait()
    for a in range(8):
        lanes = slice(128 * a, 128 * a + 128)
        total = [[None, None] for _ in range(4)]
        for k in range(NFD):
            c = cosine[k : k + 1, lanes]
            d = sine[k : k + 1, lanes]
            re = refl[0, k, :, lanes]
            im = refl[1, k, :, lanes]
            turned = (re * c - im * d, re * d + im * c)
            for g in range(4):
                for part in range(2):
                    term = turned[part] * weights[k][g]
                    total[g][part] = term if k == 0 else total[g][part] + term
        for gh in range(2):
            for part in range(2):
                core_out[gh, part, :, lanes] = total[2 * gh][part]
                core_own[gh, part, :, lanes] = total[2 * gh + 1][part]

    pl.semaphore_wait(barrier, len(first_peers))
    core_copy = pltpu.make_async_remote_copy(
        src_ref=core_out, dst_ref=core_in, send_sem=core_sem.at[0], recv_sem=core_sem.at[1],
        device_id=core_peer, device_id_type=MESH,
    )
    core_copy.start()
    for peer in x_ring:
        pl.semaphore_signal(plane_sem, inc=1, device_id=peer, device_id_type=MESH)
    loads[3].wait()
    loads[4].wait()
    core_copy.wait_recv()

    for gh in range(2):
        tiles = []
        for a in range(8):
            lanes = slice(128 * a, 128 * a + 128)
            tiles.append(tuple(core_own[gh, part, :, lanes] + core_in[gh, part, :, lanes] for part in range(2)))
        mixed = dft8(tiles)
        for k in range(8):
            vr, vi = mixed[k]
            c = twa[0, k : k + 1, :]
            d = twa[1, k : k + 1, :]
            first = gh * 128 + k * ROWS
            for part, value in enumerate((vr * c + vi * d, vi * c - vr * d)):
                hi, lo = halves(value)
                xsplit[0, first : first + ROWS, part * 128 : part * 128 + 128] = hi
                xsplit[1, first : first + ROWS, part * 128 : part * 128 + 128] = lo
    y = matmul_t(col[0], xsplit[0]) + (matmul_t(col[1], xsplit[0]) + matmul_t(col[0], xsplit[1]))
    for gh in range(2):
        for lo_index in range(2):
            y_out[gh, lo_index] = y[160 * lo_index : 160 * lo_index + 160, 128 * gh : 128 * gh + 128]

    y_copies = []
    for n, (gh, lo_index) in enumerate([(1 - y_hi, y_lo), (y_hi, 1 - y_lo), (1 - y_hi, 1 - y_lo)]):
        copy = pltpu.make_async_remote_copy(
            src_ref=y_out.at[gh, lo_index], dst_ref=y_in.at[n], send_sem=y_sem.at[0, n], recv_sem=y_sem.at[1, n],
            device_id=y_peers[n], device_id_type=MESH,
        )
        copy.start()
        y_copies.append(copy)
    pl.semaphore_wait(plane_sem, 3)
    for copy in y_copies:
        copy.wait_recv()
    low = lax.broadcasted_iota(jnp.int32, (8, 128), 0) < 4
    for t in range(20):
        rows = slice(8 * t, 8 * t + 8)
        near = y_out[y_hi, y_lo, rows, :] + y_in[0, rows, :]
        far = y_in[1, rows, :] + y_in[2, rows, :]
        b = 2 * t
        q_buf[b // 10, b % 10] = jnp.where(low, near, pltpu.roll(far, 4, 0))
        q_buf[b // 10, b % 10 + 1] = jnp.where(low, pltpu.roll(near, 4, 0), far)

    for other, peer, (px, pz) in zip(is_other, a2a_peers, dests):

        @pl.when(other)
        def _(peer=peer, px=px, pz=pz):
            pltpu.make_async_remote_copy(
                src_ref=q_buf.at[px, pl.ds(pz, 3)], dst_ref=r_buf.at[:, own], send_sem=a2a_sem.at[0],
                recv_sem=a2a_sem.at[1], device_id=peer, device_id_type=MESH,
            ).start()

    for b in range(3):
        r_buf[b, own] = q_buf[x, z + b]
    wait_bytes(r_buf.at[:, pl.ds(0, 31)], a2a_sem.at[1])

    core_copy.wait_send()
    for copy in y_copies:
        copy.wait_send()
    wait_bytes(r_buf.at[:, pl.ds(0, 31)], a2a_sem.at[0])


def finish(r_buf, widths, row_all, twb, last, sums, out_ref, rsplit, vsplit, t_buf):
    row = row_all.at[lax.rem(lax.axis_index("space") // 8, 2)]
    w_left = widths[0, 0]
    w_right = widths[0, 1]
    for b in range(3):
        hi, lo = halves(r_buf[b].reshape(256, 128))
        rsplit[0, :, 128 * b : 128 * b + 128] = hi
        rsplit[1, :, 128 * b : 128 * b + 128] = lo
    mid = matmul(row[0], rsplit[0]) + (matmul(row[1], rsplit[0]) + matmul(row[0], rsplit[1]))
    for b in range(3):
        for q in range(2):
            vr = mid[64 * q : 64 * q + 64, 128 * b : 128 * b + 128]
            vi = mid[128 + 64 * q : 192 + 64 * q, 128 * b : 128 * b + 128]
            first = (b * 2 + q) * 64
            for part, value in enumerate((vr * twb[0] + vi * twb[1], vi * twb[0] - vr * twb[1])):
                hi, lo = halves(value)
                vsplit[0, first : first + 64, 128 * part : 128 * part + 128] = hi
                vsplit[1, first : first + 64, 128 * part : 128 * part + 128] = lo
    t_buf[...] = matmul(vsplit[0], last[0]) + (matmul(vsplit[1], last[0]) + matmul(vsplit[0], last[1]))

    k_lane = lax.rem(lax.broadcasted_iota(jnp.int32, (1, 128), 1), 8)
    keep = []
    for b in range(3):
        for q in range(2):
            column = k_lane + 8 * q
            if b == 0:
                keep.append((column >= 16 - w_left).astype(F32))
            elif b == 1:
                keep.append(jnp.ones((1, 128), F32))
            else:
                keep.append((column < w_right).astype(F32))

    def block(n):
        return (t_buf[64 * n : 64 * n + 64, 0:128], t_buf[64 * n : 64 * n + 64, 128:256])

    def group_sum(value, which):
        hi, lo = halves(value)
        return matmul(jnp.concatenate([hi, lo], axis=1), sums[which])

    def normalized(nr, ni):
        both = group_sum(jnp.concatenate([nr, ni], axis=0), 0)
        vr = both[0:64]
        vi = both[64:128]
        power = vr * vr + vi * vi
        mean = jnp.sum(jnp.sum(power, axis=0, keepdims=True), axis=1, keepdims=True) * (1.0 / (8 * N))
        scale = 1.0 / jnp.sqrt(power + mean + EPS)
        return (vr * scale, vi * scale)

    nr = jnp.zeros((64, 128), F32)
    ni = jnp.zeros((64, 128), F32)
    for n in range(6):
        tr, ti = block(n)
        nr = nr + tr * keep[n]
        ni = ni + ti * keep[n]
    ur, ui = normalized(nr, ni)
    for _ in range(ITERS):
        rows = []
        for n in range(6):
            tr, ti = block(n)
            rows.append(jnp.sum(ur * tr + ui * ti, axis=0, keepdims=True) * keep[n])
            rows.append(jnp.sum(ui * tr - ur * ti, axis=0, keepdims=True) * keep[n])
        rows.append(jnp.zeros((4, 128), F32))
        back = group_sum(jnp.concatenate(rows, axis=0), 1)
        nr = jnp.zeros((64, 128), F32)
        ni = jnp.zeros((64, 128), F32)
        for n in range(6):
            tr, ti = block(n)
            br = back[2 * n : 2 * n + 1, :]
            bi = back[2 * n + 1 : 2 * n + 2, :]
            nr = nr + (tr * br - ti * bi)
            ni = ni + (tr * bi + ti * br)
        ur, ui = normalized(nr, ni)

    fixed = [[], []]
    for q in range(2):
        tr, ti = block(2 + q)
        fixed[0].append(ur * tr + ui * ti)
        fixed[1].append(ur * ti - ui * tr)
    left = lax.broadcasted_iota(jnp.int32, (8, 128), 1) < 64
    for part in range(2):
        turned = jnp.concatenate(fixed[part], axis=0).T
        for p in range(8):
            first = turned[16 * p : 16 * p + 8]
            second = turned[16 * p + 8 : 16 * p + 16]
            out_ref[part, 0:8, 128 * p : 128 * p + 128] = jnp.where(left, first, pltpu.roll(second, 64, 1))
            out_ref[part, 8:16, 128 * p : 128 * p + 128] = jnp.where(left, pltpu.roll(first, 64, 1), second)


def local(reflection, phase, group_index, widths):
    twa, col, row, twb, last, sums = [jnp.asarray(t) for t in tables()]
    anywhere = pl.BlockSpec(memory_space=pltpu.HBM)
    vmem = pl.BlockSpec(memory_space=pltpu.VMEM)
    scratch = [
        pltpu.VMEM((2, NFD, ROWS, N), F32),
        pltpu.VMEM((NFD, N), F32),
        pltpu.SMEM((NFD,), jnp.int32),
        pltpu.VMEM((2, 8, 128), F32),
        pltpu.VMEM((2, 320, 256), BF16),
        pltpu.VMEM((2, 2, ROWS, N), F32),
        pltpu.VMEM((2, 2, ROWS, N), F32),
        pltpu.VMEM((2, 2, ROWS, N), F32),
        pltpu.VMEM((2, 256, 256), BF16),
        pltpu.VMEM((2, 2, 160, 128), F32),
        pltpu.VMEM((3, 160, 128), F32),
        pltpu.VMEM((4, 10, 8, 128), F32),
        pltpu.SemaphoreType.DMA((10,)),
        pltpu.SemaphoreType.DMA((2,)),
        pltpu.SemaphoreType.DMA((2, 3)),
        pltpu.SemaphoreType.DMA((2,)),
        pltpu.SemaphoreType.REGULAR,
    ]
    gathered = pl.pallas_call(
        kernel,
        out_shape=jax.ShapeDtypeStruct((3, 32, 8, 128), F32),
        in_specs=[anywhere] * 5,
        out_specs=vmem,
        scratch_shapes=scratch,
        name="focus",
        compiler_params=pltpu.CompilerParams(
            collective_id=0, has_side_effects=True, vmem_limit_bytes=48 * 1024 * 1024
        ),
    )(*[pltpu.with_memory_space_constraint(v, pltpu.HBM) for v in (reflection, phase, group_index, twa, col)])

    result = pl.pallas_call(
        finish,
        out_shape=jax.ShapeDtypeStruct((2, ROWS, N), F32),
        in_specs=[vmem, pl.BlockSpec(memory_space=pltpu.SMEM), vmem, vmem, vmem, vmem],
        out_specs=vmem,
        scratch_shapes=[
            pltpu.VMEM((2, 256, 384), BF16),
            pltpu.VMEM((2, 384, 256), BF16),
            pltpu.VMEM((384, 256), F32),
        ],
        name="finish",
        compiler_params=pltpu.CompilerParams(vmem_limit_bytes=48 * 1024 * 1024),
    )(gathered, widths, row, twb, last, sums)
    return jnp.swapaxes(result, 1, 2)[:, None]


def solution(mesh):
    in_specs = (P(None, "freq", "space", None), P("freq", None), P("freq"), P("space", None))
    out_specs = P(None, "freq", None, "space")
    return jax.shard_map(local, mesh=mesh, in_specs=in_specs, out_specs=out_specs, check_vma=False)
```

```python
import functools
import math

import jax
import jax.numpy as jnp
import ml_dtypes
import numpy as np
from jax import lax
from jax.experimental import pallas as pl
from jax.experimental.pallas import tpu as pltpu
from jax.sharding import PartitionSpec as P

MESH = pl.DeviceIdType.MESH
F32 = jnp.float32
BF16 = jnp.bfloat16
ITERS = 3
N = 1024
NFD = 8
ROWS = 16
EPS = 1e-06


def split_np(table):
    hi = table.astype(np.float32).astype(ml_dtypes.bfloat16)
    lo = (table - hi.astype(np.float64)).astype(np.float32).astype(ml_dtypes.bfloat16)
    return np.stack([hi, lo])


def tables():
    lane = np.arange(128)
    k1 = np.arange(8)
    ang = 2 * np.pi * (k1[:, None] * lane[None, :] % N) / N
    twist_a = np.stack([np.cos(ang), np.sin(ang)]) / 32.0
    half, y_lo, x, slot, q_hi = np.meshgrid(*[np.arange(n) for n in (2, 2, 4, 5, 2)], indexing="ij")
    block = ((x * 2 + y_lo) * 8 + half * 5 + slot - 1) % 64
    k2 = (2 * block + q_hi).reshape(-1)
    ang = 2 * np.pi * (k2[:, None] * lane[None, :] % 128) / 128
    cos, sin = (np.cos(ang), np.sin(ang))
    real_rows = np.concatenate([cos, sin], axis=1)
    imag_rows = np.concatenate([-sin, cos], axis=1)
    col = np.stack([real_rows, imag_rows], axis=1).reshape(320, 256)
    row = np.zeros((2, 2, 2, 64, 4, 8, 2, 2, 2))
    m1 = np.arange(64)
    for mine in range(2):
        for rel in range(2):
            xs, zs = np.meshgrid(np.arange(4), np.arange(8), indexing="ij")
            s = (xs * 2 + (mine ^ rel)) * 8 + zs
            ang = 2 * np.pi * (m1[:, None, None] * s[None] % 64) / 64
            for q in range(2):
                row[mine, 0, q, :, :, :, rel, q, 0] = np.cos(ang)
                row[mine, 0, q, :, :, :, rel, q, 1] = np.sin(ang)
                row[mine, 1, q, :, :, :, rel, q, 0] = -np.sin(ang)
                row[mine, 1, q, :, :, :, rel, q, 1] = np.cos(ang)
    row = row.reshape(2, 256, 256)
    ang = 2 * np.pi * (m1[:, None] * (lane % 16)[None, :] % N) / N
    twist_b = np.stack([np.cos(ang), np.sin(ang)])
    last = np.zeros((2, 8, 16, 2, 16, 8))
    i, m2 = (np.arange(16), np.arange(16))
    ang = 2 * np.pi * (i[:, None] * m2[None, :] % 16) / 16
    for k in range(8):
        last[0, k, :, 0, :, k] = np.cos(ang)
        last[1, k, :, 0, :, k] = np.sin(ang)
        last[0, k, :, 1, :, k] = -np.sin(ang)
        last[1, k, :, 1, :, k] = np.cos(ang)
    last = last.reshape(256, 256) / 32.0
    over_k1 = (lane[:, None] // 8 == lane[None, :] // 8).astype(np.float64)
    over_m2 = (lane[:, None] % 8 == lane[None, :] % 8).astype(np.float64)
    sums = np.stack([np.concatenate([t, t], axis=0) for t in (over_k1, over_m2)]).astype(ml_dtypes.bfloat16)
    return (
        twist_a.astype(np.float32),
        split_np(col),
        np.moveaxis(split_np(row), 0, 1),
        twist_b.astype(np.float32),
        split_np(last),
        sums,
    )


def halves(value):
    hi = value.astype(BF16)
    lo = (value - hi.astype(F32)).astype(BF16)
    return (hi, lo)


def dft4(v):
    (ar, ai), (br, bi), (cr, ci), (dr, di) = v
    pr, pi, mr, mi = (ar + cr, ai + ci, ar - cr, ai - ci)
    qr, qi, nr, ni = (br + dr, bi + di, br - dr, bi - di)
    return [(pr + qr, pi + qi), (mr + ni, mi - nr), (pr - qr, pi - qi), (mr - ni, mi + nr)]


def dft8(v):
    even = dft4(v[0::2])
    odd = dft4(v[1::2])
    half = math.sqrt(0.5)
    o1r, o1i = odd[1]
    o2r, o2i = odd[2]
    o3r, o3i = odd[3]
    turned = [
        odd[0],
        ((o1r + o1i) * half, (o1i - o1r) * half),
        (o2i, -o2r),
        ((o3i - o3r) * half, -(o3r + o3i) * half),
    ]
    low = [(e[0] + t[0], e[1] + t[1]) for e, t in zip(even, turned)]
    high = [(e[0] - t[0], e[1] - t[1]) for e, t in zip(even, turned)]
    return low + high


def matmul(left, right):
    return jnp.dot(left, right, preferred_element_type=F32)


def matmul_t(left, right):
    return lax.dot_general(left, right, (((1,), (1,)), ((), ())), preferred_element_type=F32)


def wait_bytes(ref, sem):
    pltpu.make_async_copy(ref, ref, sem).wait()


def kernel(
    refl_hbm, phase_hbm, group_hbm, widths_hbm, twa_hbm, col_hbm, row_hbm, twb_hbm, last_hbm, sums_hbm,
    out_ref,
    refl, phase, group, widths, twa, col, row, twb, last, sums,
    core_out, core_own, core_in, xsplit, y_out, y_in, q_buf, r_buf, rsplit, vsplit, t_buf,
    load_sem, core_sem, y_sem, a2a_sem, plane_sem,
):
    f = lax.axis_index("freq")
    s = lax.axis_index("space")
    y_hi = f // 2
    core = lax.rem(f, 2)
    x = s // 16
    y_lo = lax.rem(s // 8, 2)
    z = lax.rem(s, 8)

    loads = [
        pltpu.make_async_copy(src, dst, load_sem.at[n])
        for n, (src, dst) in enumerate(
            [
                (group_hbm, group), (phase_hbm, phase), (refl_hbm, refl), (twa_hbm, twa), (col_hbm, col),
                (row_hbm.at[y_lo], row), (twb_hbm, twb), (last_hbm, last), (sums_hbm, sums), (widths_hbm, widths),
            ]
        )
    ]
    for load in loads:
        load.start()

    core_peer = (y_hi * 2 + 1 - core, s)
    other_f = (1 - y_hi) * 2 + core
    other_s = (x * 2 + 1 - y_lo) * 8 + z
    y_peers = [(other_f, s), (f, other_s), (other_f, other_s)]
    own = x * 8 + z
    dests = [(dx, pz) for pz in (0, 1, 2, 3, 4, 5, 6, 7) for dx in (2, 1, 3, 0)]

    barrier = pltpu.get_barrier_semaphore()
    z_ring = [(f, (x * 2 + y_lo) * 8 + lax.rem(z + d, 8)) for d in (4, 3, 5, 2, 6, 1, 7)]
    x_ring = [(f, (lax.rem(x + d, 4) * 2 + y_lo) * 8 + z) for d in (2, 1, 3)]
    first_peers = [core_peer] + y_peers + x_ring + z_ring
    for peer in first_peers:
        pl.semaphore_signal(barrier, inc=1, device_id=peer, device_id_type=MESH)

    loads[0].wait()
    loads[1].wait()
    angle = phase[...]
    cosine = jnp.cos(angle)
    sine = jnp.sin(angle)
    weights = [
        [(group[k] == 2 * gh + gc).astype(F32) for gh in range(2) for gc in (1 - core, core)] for k in range(NFD)
    ]
    loads[2].wait()
    for a in range(8):
        lanes = slice(128 * a, 128 * a + 128)
        total = [[None, None] for _ in range(4)]
        for k in range(NFD):
            c = cosine[k : k + 1, lanes]
            d = sine[k : k + 1, lanes]
            re = refl[0, k, :, lanes]
            im = refl[1, k, :, lanes]
            turned = (re * c - im * d, re * d + im * c)
            for g in range(4):
                for part in range(2):
                    term = turned[part] * weights[k][g]
                    total[g][part] = term if k == 0 else total[g][part] + term
        for gh in range(2):
            for part in range(2):
                core_out[gh, part, :, lanes] = total[2 * gh][part]
                core_own[gh, part, :, lanes] = total[2 * gh + 1][part]

    pl.semaphore_wait(barrier, len(first_peers))
    groups = (1 - y_hi, y_hi)
    core_copies = [
        pltpu.make_async_remote_copy(
            src_ref=core_out.at[gh], dst_ref=core_in.at[gh], send_sem=core_sem.at[0, n], recv_sem=core_sem.at[1, n],
            device_id=core_peer, device_id_type=MESH,
        )
        for n, gh in enumerate(groups)
    ]
    for copy in core_copies:
        copy.start()
    for peer in x_ring:
        pl.semaphore_signal(plane_sem, inc=1, device_id=peer, device_id_type=MESH)
    loads[3].wait()
    loads[4].wait()

    y_copies = []

    def y_part(half, n):
        rows = slice(160 * half, 160 * half + 160)
        y = matmul_t(col[0, rows], xsplit[n, 0]) + (
            matmul_t(col[1, rows], xsplit[n, 0]) + matmul_t(col[0, rows], xsplit[n, 1])
        )
        for index in range(2):
            y_out[half, n, index] = y[80 * index : 80 * index + 80]
        for place, peer in ((y_lo, y_peers[0]), (1 - y_lo, y_peers[2])) if n == 0 else ((1 - y_lo, y_peers[1]),):
            slot = len(y_copies)
            copy = pltpu.make_async_remote_copy(
                src_ref=y_out.at[half, n, place], dst_ref=y_in.at[slot], send_sem=y_sem.at[0, slot],
                recv_sem=y_sem.at[1, slot], device_id=peer, device_id_type=MESH,
            )
            copy.start()
            y_copies.append(copy)

    for n, gh in enumerate(groups):
        core_copies[n].wait_recv()
        tiles = []
        for a in range(8):
            lanes = slice(128 * a, 128 * a + 128)
            tiles.append(tuple(core_own[gh, part, :, lanes] + core_in[gh, part, :, lanes] for part in range(2)))
        mixed = dft8(tiles)
        for k in range(8):
            vr, vi = mixed[k]
            c = twa[0, k : k + 1, :]
            d = twa[1, k : k + 1, :]
            first = k * ROWS
            for part, value in enumerate((vr * c + vi * d, vi * c - vr * d)):
                hi, lo = halves(value)
                xsplit[n, 0, first : first + ROWS, part * 128 : part * 128 + 128] = hi
                xsplit[n, 1, first : first + ROWS, part * 128 : part * 128 + 128] = lo
        y_part(0, n)
    for n in range(2):
        y_part(1, n)
    pl.semaphore_wait(plane_sem, 3)

    low = lax.broadcasted_iota(jnp.int32, (8, 128), 0) < 4
    for half in range(2):
        for copy in y_copies[3 * half : 3 * half + 3]:
            copy.wait_recv()
        for t in range(10):
            rows = slice(8 * t, 8 * t + 8)
            near = y_out[half, 1, y_lo, rows, :] + y_in[3 * half, rows, :]
            far = y_in[3 * half + 1, rows, :] + y_in[3 * half + 2, rows, :]
            n = 2 * t
            q_buf[n // 5, half * 5 + n % 5] = jnp.where(low, near, pltpu.roll(far, 4, 0))
            n = n + 1
            q_buf[n // 5, half * 5 + n % 5] = jnp.where(low, pltpu.roll(near, 4, 0), far)

        for dx, pz in [d for d in dests if (d[1] >= 3) == (half == 1)]:
            px = lax.rem(x + dx, 4)

            def push(px=px, pz=pz):
                pltpu.make_async_remote_copy(
                    src_ref=q_buf.at[px, pl.ds(pz, 3)], dst_ref=r_buf.at[:, own], send_sem=a2a_sem.at[0],
                    recv_sem=a2a_sem.at[1], device_id=(f, (px * 2 + y_lo) * 8 + pz), device_id_type=MESH,
                ).start()

            if dx:
                push()
            else:
                pl.when(z != pz)(push)
    for b in range(3):
        r_buf[b, own] = q_buf[x, z + b]
    for load in loads[5:]:
        load.wait()
    w_left = widths[0, 0]
    w_right = widths[0, 1]
    wait_bytes(r_buf.at[:, pl.ds(0, 31)], a2a_sem.at[1])

    for b in range(3):
        hi, lo = halves(r_buf[b].reshape(256, 128))
        rsplit[0, :, 128 * b : 128 * b + 128] = hi
        rsplit[1, :, 128 * b : 128 * b + 128] = lo
    mid = matmul(row[0], rsplit[0]) + (matmul(row[1], rsplit[0]) + matmul(row[0], rsplit[1]))
    for b in range(3):
        for q in range(2):
            vr = mid[64 * q : 64 * q + 64, 128 * b : 128 * b + 128]
            vi = mid[128 + 64 * q : 192 + 64 * q, 128 * b : 128 * b + 128]
            first = (b * 2 + q) * 64
            for part, value in enumerate((vr * twb[0] + vi * twb[1], vi * twb[0] - vr * twb[1])):
                hi, lo = halves(value)
                vsplit[0, first : first + 64, 128 * part : 128 * part + 128] = hi
                vsplit[1, first : first + 64, 128 * part : 128 * part + 128] = lo
    t_buf[...] = matmul(vsplit[0], last[0]) + (matmul(vsplit[1], last[0]) + matmul(vsplit[0], last[1]))

    k_lane = lax.rem(lax.broadcasted_iota(jnp.int32, (1, 128), 1), 8)
    keep = []
    for b in range(3):
        for q in range(2):
            column = k_lane + 8 * q
            if b == 0:
                keep.append((column >= 16 - w_left).astype(F32))
            elif b == 1:
                keep.append(jnp.ones((1, 128), F32))
            else:
                keep.append((column < w_right).astype(F32))

    def block(n):
        return (t_buf[64 * n : 64 * n + 64, 0:128], t_buf[64 * n : 64 * n + 64, 128:256])

    def group_sum(value, which):
        hi, lo = halves(value)
        return matmul(jnp.concatenate([hi, lo], axis=1), sums[which])

    def normalized(nr, ni):
        both = group_sum(jnp.concatenate([nr, ni], axis=0), 0)
        vr = both[0:64]
        vi = both[64:128]
        power = vr * vr + vi * vi
        mean = jnp.sum(jnp.sum(power, axis=0, keepdims=True), axis=1, keepdims=True) * (1.0 / (8 * N))
        scale = 1.0 / jnp.sqrt(power + mean + EPS)
        return (vr * scale, vi * scale)

    nr = jnp.zeros((64, 128), F32)
    ni = jnp.zeros((64, 128), F32)
    for n in range(6):
        tr, ti = block(n)
        nr = nr + tr * keep[n]
        ni = ni + ti * keep[n]
    ur, ui = normalized(nr, ni)
    for _ in range(ITERS):
        rows = []
        for n in range(6):
            tr, ti = block(n)
            rows.append(jnp.sum(ur * tr + ui * ti, axis=0, keepdims=True) * keep[n])
            rows.append(jnp.sum(ui * tr - ur * ti, axis=0, keepdims=True) * keep[n])
        rows.append(jnp.zeros((4, 128), F32))
        back = group_sum(jnp.concatenate(rows, axis=0), 1)
        nr = jnp.zeros((64, 128), F32)
        ni = jnp.zeros((64, 128), F32)
        for n in range(6):
            tr, ti = block(n)
            br = back[2 * n : 2 * n + 1, :]
            bi = back[2 * n + 1 : 2 * n + 2, :]
            nr = nr + (tr * br - ti * bi)
            ni = ni + (tr * bi + ti * br)
        ur, ui = normalized(nr, ni)

    fixed = [[], []]
    for q in range(2):
        tr, ti = block(2 + q)
        fixed[0].append(ur * tr + ui * ti)
        fixed[1].append(ur * ti - ui * tr)
    left = lax.broadcasted_iota(jnp.int32, (8, 128), 1) < 64
    for part in range(2):
        turned = jnp.concatenate(fixed[part], axis=0).T
        for p in range(8):
            first = turned[16 * p : 16 * p + 8]
            second = turned[16 * p + 8 : 16 * p + 16]
            out_ref[part, 0:8, 128 * p : 128 * p + 128] = jnp.where(left, first, pltpu.roll(second, 64, 1))
            out_ref[part, 8:16, 128 * p : 128 * p + 128] = jnp.where(left, pltpu.roll(first, 64, 1), second)

    for copy in core_copies + y_copies:
        copy.wait_send()
    wait_bytes(r_buf.at[:, pl.ds(0, 31)], a2a_sem.at[0])


def local(reflection, phase, group_index, widths):
    consts = [jnp.asarray(t) for t in tables()]
    operands = [reflection, phase, group_index, widths] + consts
    operands = [pltpu.with_memory_space_constraint(v, pltpu.HBM) for v in operands]
    in_specs = [pl.BlockSpec(memory_space=pltpu.HBM)] * len(operands)
    scratch = [
        pltpu.VMEM((2, NFD, ROWS, N), F32),
        pltpu.VMEM((NFD, N), F32),
        pltpu.SMEM((NFD,), jnp.int32),
        pltpu.SMEM((1, 2), jnp.int32),
        pltpu.VMEM((2, 8, 128), F32),
        pltpu.VMEM((2, 320, 256), BF16),
        pltpu.VMEM((2, 256, 256), BF16),
        pltpu.VMEM((2, 64, 128), F32),
        pltpu.VMEM((2, 256, 256), BF16),
        pltpu.VMEM((2, 256, 128), BF16),
        pltpu.VMEM((2, 2, ROWS, N), F32),
        pltpu.VMEM((2, 2, ROWS, N), F32),
        pltpu.VMEM((2, 2, ROWS, N), F32),
        pltpu.VMEM((2, 2, 128, 256), BF16),
        pltpu.VMEM((2, 2, 2, 80, 128), F32),
        pltpu.VMEM((6, 80, 128), F32),
        pltpu.VMEM((4, 10, 8, 128), F32),
        pltpu.VMEM((3, 32, 8, 128), F32),
        pltpu.VMEM((2, 256, 384), BF16),
        pltpu.VMEM((2, 384, 256), BF16),
        pltpu.VMEM((384, 256), F32),
        pltpu.SemaphoreType.DMA((10,)),
        pltpu.SemaphoreType.DMA((2, 2)),
        pltpu.SemaphoreType.DMA((2, 6)),
        pltpu.SemaphoreType.DMA((2,)),
        pltpu.SemaphoreType.REGULAR,
    ]
    result = pl.pallas_call(
        kernel,
        out_shape=jax.ShapeDtypeStruct((2, ROWS, N), F32),
        in_specs=in_specs,
        out_specs=pl.BlockSpec(memory_space=pltpu.VMEM),
        scratch_shapes=scratch,
        name="focus",
        compiler_params=pltpu.CompilerParams(
            collective_id=0, has_side_effects=True, vmem_limit_bytes=48 * 1024 * 1024
        ),
    )(*operands)
    return jnp.swapaxes(result, 1, 2)[:, None]


def solution(mesh):
    in_specs = (P(None, "freq", "space", None), P("freq", None), P("freq"), P("space", None))
    out_specs = P(None, "freq", None, "space")
    return jax.shard_map(local, mesh=mesh, in_specs=in_specs, out_specs=out_specs, check_vma=False)
```

```python
import functools
import math

import jax
import jax.numpy as jnp
import ml_dtypes
import numpy as np
from jax import lax
from jax.experimental import pallas as pl
from jax.experimental.pallas import tpu as pltpu
from jax.sharding import PartitionSpec as P

MESH = pl.DeviceIdType.MESH
F32 = jnp.float32
BF16 = jnp.bfloat16
ITERS = 3
N = 1024
NFD = 8
ROWS = 16
EPS = 1e-06
CHUNKS = ((0, 3), (3, 2), (5, 2), (7, 3))


def split_np(table):
    hi = table.astype(np.float32).astype(ml_dtypes.bfloat16)
    lo = (table - hi.astype(np.float64)).astype(np.float32).astype(ml_dtypes.bfloat16)
    return np.stack([hi, lo])


def tables():
    lane = np.arange(128)
    k1 = np.arange(8)
    ang = 2 * np.pi * (k1[:, None] * lane[None, :] % N) / N
    twist_a = np.stack([np.cos(ang), np.sin(ang)]) / 32.0
    k2 = []
    for first, count in CHUNKS:
        y_lo, x, slot, q_hi = np.meshgrid(np.arange(2), np.arange(4), first + np.arange(count), np.arange(2), indexing="ij")
        k2.append((2 * (((x * 2 + y_lo) * 8 + slot - 1) % 64) + q_hi).reshape(-1))
    k2 = np.concatenate(k2)
    ang = 2 * np.pi * (k2[:, None] * lane[None, :] % 128) / 128
    cos, sin = (np.cos(ang), np.sin(ang))
    real_rows = np.concatenate([cos, sin], axis=1)
    imag_rows = np.concatenate([-sin, cos], axis=1)
    col = np.stack([real_rows, imag_rows], axis=1).reshape(320, 256)
    row = np.zeros((2, 2, 2, 64, 4, 8, 2, 2, 2))
    m1 = np.arange(64)
    for mine in range(2):
        for rel in range(2):
            xs, zs = np.meshgrid(np.arange(4), np.arange(8), indexing="ij")
            s = (xs * 2 + (mine ^ rel)) * 8 + zs
            ang = 2 * np.pi * (m1[:, None, None] * s[None] % 64) / 64
            for q in range(2):
                row[mine, 0, q, :, :, :, rel, q, 0] = np.cos(ang)
                row[mine, 0, q, :, :, :, rel, q, 1] = np.sin(ang)
                row[mine, 1, q, :, :, :, rel, q, 0] = -np.sin(ang)
                row[mine, 1, q, :, :, :, rel, q, 1] = np.cos(ang)
    row = row.reshape(2, 256, 256)
    ang = 2 * np.pi * (m1[:, None] * (lane % 16)[None, :] % N) / N
    twist_b = np.stack([np.cos(ang), np.sin(ang)])
    last = np.zeros((2, 8, 16, 2, 16, 8))
    i, m2 = (np.arange(16), np.arange(16))
    ang = 2 * np.pi * (i[:, None] * m2[None, :] % 16) / 16
    for k in range(8):
        last[0, k, :, 0, :, k] = np.cos(ang)
        last[1, k, :, 0, :, k] = np.sin(ang)
        last[0, k, :, 1, :, k] = -np.sin(ang)
        last[1, k, :, 1, :, k] = np.cos(ang)
    last = last.reshape(256, 256) / 32.0
    over_k1 = (lane[:, None] // 8 == lane[None, :] // 8).astype(np.float64)
    over_m2 = (lane[:, None] % 8 == lane[None, :] % 8).astype(np.float64)
    sums = np.stack([np.concatenate([t, t], axis=0) for t in (over_k1, over_m2)]).astype(ml_dtypes.bfloat16)
    return (
        twist_a.astype(np.float32),
        split_np(col),
        np.moveaxis(split_np(row), 0, 1),
        twist_b.astype(np.float32),
        split_np(last),
        sums,
    )


def halves(value):
    hi = value.astype(BF16)
    lo = (value - hi.astype(F32)).astype(BF16)
    return (hi, lo)


def dft4(v):
    (ar, ai), (br, bi), (cr, ci), (dr, di) = v
    pr, pi, mr, mi = (ar + cr, ai + ci, ar - cr, ai - ci)
    qr, qi, nr, ni = (br + dr, bi + di, br - dr, bi - di)
    return [(pr + qr, pi + qi), (mr + ni, mi - nr), (pr - qr, pi - qi), (mr - ni, mi + nr)]


def dft8(v):
    even = dft4(v[0::2])
    odd = dft4(v[1::2])
    half = math.sqrt(0.5)
    o1r, o1i = odd[1]
    o2r, o2i = odd[2]
    o3r, o3i = odd[3]
    turned = [
        odd[0],
        ((o1r + o1i) * half, (o1i - o1r) * half),
        (o2i, -o2r),
        ((o3i - o3r) * half, -(o3r + o3i) * half),
    ]
    low = [(e[0] + t[0], e[1] + t[1]) for e, t in zip(even, turned)]
    high = [(e[0] - t[0], e[1] - t[1]) for e, t in zip(even, turned)]
    return low + high


def matmul(left, right):
    return jnp.dot(left, right, preferred_element_type=F32)


def matmul_t(left, right):
    return lax.dot_general(left, right, (((1,), (1,)), ((), ())), preferred_element_type=F32)


def wait_bytes(ref, sem):
    pltpu.make_async_copy(ref, ref, sem).wait()


def kernel(
    refl_hbm, phase_hbm, group_hbm, widths_hbm, twa_hbm, col_hbm, row_hbm, twb_hbm, last_hbm, sums_hbm,
    out_ref,
    refl, phase, group, widths, twa, col, row, twb, last, sums,
    core_out, core_own, core_in, xsplit, y_out, y_in, q_buf, r_buf, rsplit, vsplit, t_buf,
    load_sem, core_sem, y_sem, a2a_sem, plane_sem,
):
    f = lax.axis_index("freq")
    s = lax.axis_index("space")
    y_hi = f // 2
    core = lax.rem(f, 2)
    x = s // 16
    y_lo = lax.rem(s // 8, 2)
    z = lax.rem(s, 8)

    loads = [
        pltpu.make_async_copy(src, dst, load_sem.at[n])
        for n, (src, dst) in enumerate(
            [
                (group_hbm, group), (phase_hbm, phase), (refl_hbm, refl), (twa_hbm, twa), (col_hbm, col),
                (row_hbm.at[y_lo], row), (twb_hbm, twb), (last_hbm, last), (sums_hbm, sums), (widths_hbm, widths),
            ]
        )
    ]
    for load in loads:
        load.start()

    core_peer = (y_hi * 2 + 1 - core, s)
    other_f = (1 - y_hi) * 2 + core
    other_s = (x * 2 + 1 - y_lo) * 8 + z
    y_peers = [(other_f, s), (f, other_s), (other_f, other_s)]
    own = x * 8 + z
    dests = [(dx, pz) for pz in (0, 1, 2, 3, 4, 5, 6, 7) for dx in (2, 1, 3, 0)]

    barrier = pltpu.get_barrier_semaphore()
    z_ring = [(f, (x * 2 + y_lo) * 8 + lax.rem(z + d, 8)) for d in (4, 3, 5, 2, 6, 1, 7)]
    x_ring = [(f, (lax.rem(x + d, 4) * 2 + y_lo) * 8 + z) for d in (2, 1, 3)]
    first_peers = [core_peer] + y_peers + x_ring + z_ring
    for peer in first_peers:
        pl.semaphore_signal(barrier, inc=1, device_id=peer, device_id_type=MESH)

    loads[0].wait()
    loads[1].wait()
    angle = phase[...]
    cosine = jnp.cos(angle)
    sine = jnp.sin(angle)
    weights = [
        [(group[k] == 2 * gh + gc).astype(F32) for gh in range(2) for gc in (1 - core, core)] for k in range(NFD)
    ]
    loads[2].wait()
    for a in range(8):
        lanes = slice(128 * a, 128 * a + 128)
        total = [[None, None] for _ in range(4)]
        for k in range(NFD):
            c = cosine[k : k + 1, lanes]
            d = sine[k : k + 1, lanes]
            re = refl[0, k, :, lanes]
            im = refl[1, k, :, lanes]
            turned = (re * c - im * d, re * d + im * c)
            for g in range(4):
                for part in range(2):
                    term = turned[part] * weights[k][g]
                    total[g][part] = term if k == 0 else total[g][part] + term
        for gh in range(2):
            for part in range(2):
                core_out[gh, part, :, lanes] = total[2 * gh][part]
                core_own[gh, part, :, lanes] = total[2 * gh + 1][part]

    pl.semaphore_wait(barrier, len(first_peers))
    groups = (1 - y_hi, y_hi)
    core_copies = [
        pltpu.make_async_remote_copy(
            src_ref=core_out.at[gh], dst_ref=core_in.at[gh], send_sem=core_sem.at[0, n], recv_sem=core_sem.at[1, n],
            device_id=core_peer, device_id_type=MESH,
        )
        for n, gh in enumerate(groups)
    ]
    for copy in core_copies:
        copy.start()
    for peer in x_ring:
        pl.semaphore_signal(plane_sem, inc=1, device_id=peer, device_id_type=MESH)
    loads[3].wait()
    loads[4].wait()

    y_copies = []

    def y_part(half, n):
        first, count = CHUNKS[half]
        rows = slice(32 * first, 32 * (first + count))
        y = matmul_t(col[0, rows], xsplit[n, 0]) + (
            matmul_t(col[1, rows], xsplit[n, 0]) + matmul_t(col[0, rows], xsplit[n, 1])
        )
        for index in range(2):
            y_out[n, index, 16 * first : 16 * (first + count)] = y[16 * count * index : 16 * count * (index + 1)]
        for place, peer in ((y_lo, y_peers[0]), (1 - y_lo, y_peers[2])) if n == 0 else ((1 - y_lo, y_peers[1]),):
            slot = len(y_copies)
            part = pl.ds(16 * first, 16 * count)
            copy = pltpu.make_async_remote_copy(
                src_ref=y_out.at[n, place, part], dst_ref=y_in.at[slot % 3, part], send_sem=y_sem.at[0, slot],
                recv_sem=y_sem.at[1, slot], device_id=peer, device_id_type=MESH,
            )
            copy.start()
            y_copies.append(copy)

    for n, gh in enumerate(groups):
        core_copies[n].wait_recv()
        tiles = []
        for a in range(8):
            lanes = slice(128 * a, 128 * a + 128)
            tiles.append(tuple(core_own[gh, part, :, lanes] + core_in[gh, part, :, lanes] for part in range(2)))
        mixed = dft8(tiles)
        for k in range(8):
            vr, vi = mixed[k]
            c = twa[0, k : k + 1, :]
            d = twa[1, k : k + 1, :]
            first = k * ROWS
            for part, value in enumerate((vr * c + vi * d, vi * c - vr * d)):
                hi, lo = halves(value)
                xsplit[n, 0, first : first + ROWS, part * 128 : part * 128 + 128] = hi
                xsplit[n, 1, first : first + ROWS, part * 128 : part * 128 + 128] = lo
        y_part(0, n)
    for half in range(1, len(CHUNKS)):
        for n in range(2):
            y_part(half, n)
    pl.semaphore_wait(plane_sem, 3)

    low = lax.broadcasted_iota(jnp.int32, (8, 128), 0) < 4
    for half, (first, count) in enumerate(CHUNKS):
        for copy in y_copies[3 * half : 3 * half + 3]:
            copy.wait_recv()
        for t in range(2 * count):
            rows = slice(16 * first + 8 * t, 16 * first + 8 * t + 8)
            near = y_out[1, y_lo, rows, :] + y_in[0, rows, :]
            far = y_in[1, rows, :] + y_in[2, rows, :]
            n = 2 * t
            q_buf[n // count, first + n % count] = jnp.where(low, near, pltpu.roll(far, 4, 0))
            n = n + 1
            q_buf[n // count, first + n % count] = jnp.where(low, pltpu.roll(near, 4, 0), far)

        for dx, pz in [d for d in dests if first <= d[1] + 2 < first + count]:
            px = lax.rem(x + dx, 4)

            def push(px=px, pz=pz):
                pltpu.make_async_remote_copy(
                    src_ref=q_buf.at[px, pl.ds(pz, 3)], dst_ref=r_buf.at[:, own], send_sem=a2a_sem.at[0],
                    recv_sem=a2a_sem.at[1], device_id=(f, (px * 2 + y_lo) * 8 + pz), device_id_type=MESH,
                ).start()

            if dx:
                push()
            else:
                pl.when(z != pz)(push)
    for b in range(3):
        r_buf[b, own] = q_buf[x, z + b]
    for load in loads[5:]:
        load.wait()
    w_left = widths[0, 0]
    w_right = widths[0, 1]
    wait_bytes(r_buf.at[:, pl.ds(0, 31)], a2a_sem.at[1])

    for b in range(3):
        hi, lo = halves(r_buf[b].reshape(256, 128))
        rsplit[0, :, 128 * b : 128 * b + 128] = hi
        rsplit[1, :, 128 * b : 128 * b + 128] = lo
    mid = matmul(row[0], rsplit[0]) + (matmul(row[1], rsplit[0]) + matmul(row[0], rsplit[1]))
    for b in range(3):
        for q in range(2):
            vr = mid[64 * q : 64 * q + 64, 128 * b : 128 * b + 128]
            vi = mid[128 + 64 * q : 192 + 64 * q, 128 * b : 128 * b + 128]
            first = (b * 2 + q) * 64
            for part, value in enumerate((vr * twb[0] + vi * twb[1], vi * twb[0] - vr * twb[1])):
                hi, lo = halves(value)
                vsplit[0, first : first + 64, 128 * part : 128 * part + 128] = hi
                vsplit[1, first : first + 64, 128 * part : 128 * part + 128] = lo
    t_buf[...] = matmul(vsplit[0], last[0]) + (matmul(vsplit[1], last[0]) + matmul(vsplit[0], last[1]))

    k_lane = lax.rem(lax.broadcasted_iota(jnp.int32, (1, 128), 1), 8)
    keep = []
    for b in range(3):
        for q in range(2):
            column = k_lane + 8 * q
            if b == 0:
                keep.append((column >= 16 - w_left).astype(F32))
            elif b == 1:
                keep.append(jnp.ones((1, 128), F32))
            else:
                keep.append((column < w_right).astype(F32))

    def block(n):
        return (t_buf[64 * n : 64 * n + 64, 0:128], t_buf[64 * n : 64 * n + 64, 128:256])

    def group_sum(value, which):
        hi, lo = halves(value)
        return matmul(jnp.concatenate([hi, lo], axis=1), sums[which])

    def normalized(nr, ni):
        both = group_sum(jnp.concatenate([nr, ni], axis=0), 0)
        vr = both[0:64]
        vi = both[64:128]
        power = vr * vr + vi * vi
        mean = jnp.sum(jnp.sum(power, axis=0, keepdims=True), axis=1, keepdims=True) * (1.0 / (8 * N))
        scale = 1.0 / jnp.sqrt(power + mean + EPS)
        return (vr * scale, vi * scale)

    nr = jnp.zeros((64, 128), F32)
    ni = jnp.zeros((64, 128), F32)
    for n in range(6):
        tr, ti = block(n)
        nr = nr + tr * keep[n]
        ni = ni + ti * keep[n]
    ur, ui = normalized(nr, ni)
    for _ in range(ITERS):
        rows = []
        for n in range(6):
            tr, ti = block(n)
            rows.append(jnp.sum(ur * tr + ui * ti, axis=0, keepdims=True) * keep[n])
            rows.append(jnp.sum(ui * tr - ur * ti, axis=0, keepdims=True) * keep[n])
        rows.append(jnp.zeros((4, 128), F32))
        back = group_sum(jnp.concatenate(rows, axis=0), 1)
        nr = jnp.zeros((64, 128), F32)
        ni = jnp.zeros((64, 128), F32)
        for n in range(6):
            tr, ti = block(n)
            br = back[2 * n : 2 * n + 1, :]
            bi = back[2 * n + 1 : 2 * n + 2, :]
            nr = nr + (tr * br - ti * bi)
            ni = ni + (tr * bi + ti * br)
        ur, ui = normalized(nr, ni)

    fixed = [[], []]
    for q in range(2):
        tr, ti = block(2 + q)
        fixed[0].append(ur * tr + ui * ti)
        fixed[1].append(ur * ti - ui * tr)
    left = lax.broadcasted_iota(jnp.int32, (8, 128), 1) < 64
    for part in range(2):
        turned = jnp.concatenate(fixed[part], axis=0).T
        for p in range(8):
            first = turned[16 * p : 16 * p + 8]
            second = turned[16 * p + 8 : 16 * p + 16]
            out_ref[part, 0:8, 128 * p : 128 * p + 128] = jnp.where(left, first, pltpu.roll(second, 64, 1))
            out_ref[part, 8:16, 128 * p : 128 * p + 128] = jnp.where(left, pltpu.roll(first, 64, 1), second)

    for copy in core_copies + y_copies:
        copy.wait_send()
    wait_bytes(r_buf.at[:, pl.ds(0, 31)], a2a_sem.at[0])


def local(reflection, phase, group_index, widths):
    consts = [jnp.asarray(t) for t in tables()]
    operands = [reflection, phase, group_index, widths] + consts
    operands = [pltpu.with_memory_space_constraint(v, pltpu.HBM) for v in operands]
    in_specs = [pl.BlockSpec(memory_space=pltpu.HBM)] * len(operands)
    scratch = [
        pltpu.VMEM((2, NFD, ROWS, N), F32),
        pltpu.VMEM((NFD, N), F32),
        pltpu.SMEM((NFD,), jnp.int32),
        pltpu.SMEM((1, 2), jnp.int32),
        pltpu.VMEM((2, 8, 128), F32),
        pltpu.VMEM((2, 320, 256), BF16),
        pltpu.VMEM((2, 256, 256), BF16),
        pltpu.VMEM((2, 64, 128), F32),
        pltpu.VMEM((2, 256, 256), BF16),
        pltpu.VMEM((2, 256, 128), BF16),
        pltpu.VMEM((2, 2, ROWS, N), F32),
        pltpu.VMEM((2, 2, ROWS, N), F32),
        pltpu.VMEM((2, 2, ROWS, N), F32),
        pltpu.VMEM((2, 2, 128, 256), BF16),
        pltpu.VMEM((2, 2, 160, 128), F32),
        pltpu.VMEM((3, 160, 128), F32),
        pltpu.VMEM((4, 10, 8, 128), F32),
        pltpu.VMEM((3, 32, 8, 128), F32),
        pltpu.VMEM((2, 256, 384), BF16),
        pltpu.VMEM((2, 384, 256), BF16),
        pltpu.VMEM((384, 256), F32),
        pltpu.SemaphoreType.DMA((10,)),
        pltpu.SemaphoreType.DMA((2, 2)),
        pltpu.SemaphoreType.DMA((2, 3 * len(CHUNKS))),
        pltpu.SemaphoreType.DMA((2,)),
        pltpu.SemaphoreType.REGULAR,
    ]
    result = pl.pallas_call(
        kernel,
        out_shape=jax.ShapeDtypeStruct((2, ROWS, N), F32),
        in_specs=in_specs,
        out_specs=pl.BlockSpec(memory_space=pltpu.VMEM),
        scratch_shapes=scratch,
        name="focus",
        compiler_params=pltpu.CompilerParams(
            collective_id=0, has_side_effects=True, vmem_limit_bytes=48 * 1024 * 1024
        ),
    )(*operands)
    return jnp.swapaxes(result, 1, 2)[:, None]


def solution(mesh):
    in_specs = (P(None, "freq", "space", None), P("freq", None), P("freq"), P("space", None))
    out_specs = P(None, "freq", None, "space")
    return jax.shard_map(local, mesh=mesh, in_specs=in_specs, out_specs=out_specs, check_vma=False)
```

```python
import functools
import math

import jax
import jax.numpy as jnp
import ml_dtypes
import numpy as np
from jax import lax
from jax.experimental import pallas as pl
from jax.experimental.pallas import tpu as pltpu
from jax.sharding import PartitionSpec as P

MESH = pl.DeviceIdType.MESH
F32 = jnp.float32
BF16 = jnp.bfloat16
ITERS = 3
N = 1024
NFD = 8
ROWS = 16
EPS = 1e-06
CHUNKS = ((0, 3), (3, 2), (5, 2), (7, 3))


def split_np(table):
    hi = table.astype(np.float32).astype(ml_dtypes.bfloat16)
    lo = (table - hi.astype(np.float64)).astype(np.float32).astype(ml_dtypes.bfloat16)
    return np.stack([hi, lo])


def tables():
    lane = np.arange(128)
    k1 = np.arange(8)
    ang = 2 * np.pi * (k1[:, None] * lane[None, :] % N) / N
    twist_a = np.stack([np.cos(ang), np.sin(ang)]) / 32.0
    k2 = []
    for first, count in CHUNKS:
        y_lo, x, slot, q_hi = np.meshgrid(np.arange(2), np.arange(4), first + np.arange(count), np.arange(2), indexing="ij")
        k2.append((2 * (((x * 2 + y_lo) * 8 + slot - 1) % 64) + q_hi).reshape(-1))
    k2 = np.concatenate(k2)
    ang = 2 * np.pi * (k2[:, None] * lane[None, :] % 128) / 128
    cos, sin = (np.cos(ang), np.sin(ang))
    real_rows = np.concatenate([cos, sin], axis=1)
    imag_rows = np.concatenate([-sin, cos], axis=1)
    col = np.stack([real_rows, imag_rows], axis=1).reshape(320, 256)
    row = np.zeros((2, 2, 2, 64, 4, 8, 2, 2, 2))
    m1 = np.arange(64)
    for mine in range(2):
        for rel in range(2):
            xs, zs = np.meshgrid(np.arange(4), np.arange(8), indexing="ij")
            s = (xs * 2 + (mine ^ rel)) * 8 + zs
            ang = 2 * np.pi * (m1[:, None, None] * s[None] % 64) / 64
            for q in range(2):
                row[mine, 0, q, :, :, :, rel, q, 0] = np.cos(ang)
                row[mine, 0, q, :, :, :, rel, q, 1] = np.sin(ang)
                row[mine, 1, q, :, :, :, rel, q, 0] = -np.sin(ang)
                row[mine, 1, q, :, :, :, rel, q, 1] = np.cos(ang)
    row = row.reshape(2, 256, 256)
    ang = 2 * np.pi * (m1[:, None] * (lane % 16)[None, :] % N) / N
    twist_b = np.stack([np.cos(ang), np.sin(ang)])
    last = np.zeros((2, 8, 16, 2, 16, 8))
    i, m2 = (np.arange(16), np.arange(16))
    ang = 2 * np.pi * (i[:, None] * m2[None, :] % 16) / 16
    for k in range(8):
        last[0, k, :, 0, :, k] = np.cos(ang)
        last[1, k, :, 0, :, k] = np.sin(ang)
        last[0, k, :, 1, :, k] = -np.sin(ang)
        last[1, k, :, 1, :, k] = np.cos(ang)
    last = last.reshape(256, 256) / 32.0
    over_k1 = (lane[:, None] // 8 == lane[None, :] // 8).astype(np.float64)
    over_m2 = (lane[:, None] % 8 == lane[None, :] % 8).astype(np.float64)
    sums = np.stack([np.concatenate([t, t], axis=0) for t in (over_k1, over_m2)]).astype(ml_dtypes.bfloat16)
    return (
        twist_a.astype(np.float32),
        split_np(col),
        np.moveaxis(split_np(row), 0, 1),
        twist_b.astype(np.float32),
        split_np(last),
        sums,
    )


def halves(value):
    hi = value.astype(BF16)
    lo = (value - hi.astype(F32)).astype(BF16)
    return (hi, lo)


def dft4(v):
    (ar, ai), (br, bi), (cr, ci), (dr, di) = v
    pr, pi, mr, mi = (ar + cr, ai + ci, ar - cr, ai - ci)
    qr, qi, nr, ni = (br + dr, bi + di, br - dr, bi - di)
    return [(pr + qr, pi + qi), (mr + ni, mi - nr), (pr - qr, pi - qi), (mr - ni, mi + nr)]


def dft8(v):
    even = dft4(v[0::2])
    odd = dft4(v[1::2])
    half = math.sqrt(0.5)
    o1r, o1i = odd[1]
    o2r, o2i = odd[2]
    o3r, o3i = odd[3]
    turned = [
        odd[0],
        ((o1r + o1i) * half, (o1i - o1r) * half),
        (o2i, -o2r),
        ((o3i - o3r) * half, -(o3r + o3i) * half),
    ]
    low = [(e[0] + t[0], e[1] + t[1]) for e, t in zip(even, turned)]
    high = [(e[0] - t[0], e[1] - t[1]) for e, t in zip(even, turned)]
    return low + high


def matmul(left, right):
    return jnp.dot(left, right, preferred_element_type=F32)


def matmul_t(left, right):
    return lax.dot_general(left, right, (((1,), (1,)), ((), ())), preferred_element_type=F32)


def wait_bytes(ref, sem):
    pltpu.make_async_copy(ref, ref, sem).wait()


def kernel(
    refl_hbm, phase_hbm, group_hbm, widths_hbm, twa_hbm, col_hbm, row_hbm, twb_hbm, last_hbm, sums_hbm,
    out_ref,
    refl, phase, group, widths, twa, col, row, twb, last, sums,
    core_out, core_own, core_in, xsplit, y_out, y_in, q_buf, r_buf, rsplit, vsplit, t_buf,
    load_sem, core_sem, y_sem, a2a_sem, plane_sem,
):
    f = lax.axis_index("freq")
    s = lax.axis_index("space")
    y_hi = f // 2
    core = lax.rem(f, 2)
    x = s // 16
    y_lo = lax.rem(s // 8, 2)
    z = lax.rem(s, 8)

    core_peer = (y_hi * 2 + 1 - core, s)
    other_f = (1 - y_hi) * 2 + core
    other_s = (x * 2 + 1 - y_lo) * 8 + z
    y_peers = [(other_f, s), (f, other_s), (other_f, other_s)]
    own = x * 8 + z

    barrier = pltpu.get_barrier_semaphore()
    z_ring = [(f, (x * 2 + y_lo) * 8 + lax.rem(z + d, 8)) for d in (4, 3, 5, 2, 6, 1, 7)]
    x_ring = [(f, (lax.rem(x + d, 4) * 2 + y_lo) * 8 + z) for d in (2, 1, 3)]
    first_peers = z_ring[:3] + y_peers[:1] + x_ring[:1] + z_ring[3:] + y_peers[1:] + x_ring[1:] + [core_peer]
    for peer in first_peers:
        pl.semaphore_signal(barrier, inc=1, device_id=peer, device_id_type=MESH)

    loads = [
        pltpu.make_async_copy(src, dst, load_sem.at[n])
        for n, (src, dst) in enumerate(
            [
                (group_hbm, group), (phase_hbm, phase), (refl_hbm, refl), (twa_hbm, twa), (col_hbm, col),
                (row_hbm.at[y_lo], row), (twb_hbm, twb), (last_hbm, last), (sums_hbm, sums), (widths_hbm, widths),
            ]
        )
    ]
    for load in loads:
        load.start()

    loads[0].wait()
    loads[1].wait()
    angle = phase[...]
    cosine = jnp.cos(angle)
    sine = jnp.sin(angle)
    weights = [
        [(group[k] == 2 * gh + gc).astype(F32) for gh in range(2) for gc in (1 - core, core)] for k in range(NFD)
    ]
    loads[2].wait()
    for a in range(8):
        lanes = slice(128 * a, 128 * a + 128)
        total = [[None, None] for _ in range(4)]
        for k in range(NFD):
            c = cosine[k : k + 1, lanes]
            d = sine[k : k + 1, lanes]
            re = refl[0, k, :, lanes]
            im = refl[1, k, :, lanes]
            turned = (re * c - im * d, re * d + im * c)
            for g in range(4):
                for part in range(2):
                    term = turned[part] * weights[k][g]
                    total[g][part] = term if k == 0 else total[g][part] + term
        for gh in range(2):
            for part in range(2):
                core_out[gh, part, :, lanes] = total[2 * gh][part]
                core_own[gh, part, :, lanes] = total[2 * gh + 1][part]

    pl.semaphore_wait(barrier, len(first_peers))
    groups = (1 - y_hi, y_hi)
    core_copies = [
        pltpu.make_async_remote_copy(
            src_ref=core_out.at[gh], dst_ref=core_in.at[gh], send_sem=core_sem.at[0, n], recv_sem=core_sem.at[1, n],
            device_id=core_peer, device_id_type=MESH,
        )
        for n, gh in enumerate(groups)
    ]
    for copy in core_copies:
        copy.start()
    for peer in x_ring:
        pl.semaphore_signal(plane_sem, inc=1, device_id=peer, device_id_type=MESH)
    loads[3].wait()
    loads[4].wait()

    y_copies = []

    def y_part(half, n):
        first, count = CHUNKS[half]
        rows = slice(32 * first, 32 * (first + count))
        y = matmul_t(col[0, rows], xsplit[n, 0]) + (
            matmul_t(col[1, rows], xsplit[n, 0]) + matmul_t(col[0, rows], xsplit[n, 1])
        )
        for index in range(2):
            y_out[n, index, 16 * first : 16 * (first + count)] = y[16 * count * index : 16 * count * (index + 1)]
        for place, peer in ((y_lo, y_peers[0]), (1 - y_lo, y_peers[2])) if n == 0 else ((1 - y_lo, y_peers[1]),):
            slot = len(y_copies)
            part = pl.ds(16 * first, 16 * count)
            copy = pltpu.make_async_remote_copy(
                src_ref=y_out.at[n, place, part], dst_ref=y_in.at[slot % 3, part], send_sem=y_sem.at[0, slot],
                recv_sem=y_sem.at[1, slot], device_id=peer, device_id_type=MESH,
            )
            copy.start()
            y_copies.append(copy)

    for n, gh in enumerate(groups):
        core_copies[n].wait_recv()
        tiles = []
        for a in range(8):
            lanes = slice(128 * a, 128 * a + 128)
            tiles.append(tuple(core_own[gh, part, :, lanes] + core_in[gh, part, :, lanes] for part in range(2)))
        mixed = dft8(tiles)
        for k in range(8):
            vr, vi = mixed[k]
            c = twa[0, k : k + 1, :]
            d = twa[1, k : k + 1, :]
            first = k * ROWS
            for part, value in enumerate((vr * c + vi * d, vi * c - vr * d)):
                hi, lo = halves(value)
                xsplit[n, 0, first : first + ROWS, part * 128 : part * 128 + 128] = hi
                xsplit[n, 1, first : first + ROWS, part * 128 : part * 128 + 128] = lo
        y_part(0, n)
    for half in range(1, len(CHUNKS)):
        for n in range(2):
            y_part(half, n)
    pl.semaphore_wait(plane_sem, 3)

    low = lax.broadcasted_iota(jnp.int32, (8, 128), 0) < 4
    for half, (first, count) in enumerate(CHUNKS):
        for copy in y_copies[3 * half : 3 * half + 3]:
            copy.wait_recv()
        for t in range(2 * count):
            rows = slice(16 * first + 8 * t, 16 * first + 8 * t + 8)
            near = y_out[1, y_lo, rows, :] + y_in[0, rows, :]
            far = y_in[1, rows, :] + y_in[2, rows, :]
            n = 2 * t
            q_buf[n // count, first + n % count] = jnp.where(low, near, pltpu.roll(far, 4, 0))
            n = n + 1
            q_buf[n // count, first + n % count] = jnp.where(low, pltpu.roll(near, 4, 0), far)

        now = [pz for pz in range(8) if first <= pz + 2 < first + count]
        for dx, pz in [(None, pz) for pz in now] + [(dx, pz) for pz in now for dx in (2, 1, 3, 0)]:
            px = 0 if dx is None else lax.rem(x + dx, 4)

            def push(px=px, pz=pz):
                pltpu.make_async_remote_copy(
                    src_ref=q_buf.at[px, pl.ds(pz, 3)], dst_ref=r_buf.at[:, own], send_sem=a2a_sem.at[0],
                    recv_sem=a2a_sem.at[1], device_id=(f, (px * 2 + y_lo) * 8 + pz), device_id_type=MESH,
                ).start()

            other = own != px * 8 + pz
            pl.when(other if dx is None else jnp.logical_and(px != 0, other))(push)
    for b in range(3):
        r_buf[b, own] = q_buf[x, z + b]
    for load in loads[5:]:
        load.wait()
    w_left = widths[0, 0]
    w_right = widths[0, 1]
    wait_bytes(r_buf.at[:, pl.ds(0, 31)], a2a_sem.at[1])

    for b in range(3):
        hi, lo = halves(r_buf[b].reshape(256, 128))
        rsplit[0, :, 128 * b : 128 * b + 128] = hi
        rsplit[1, :, 128 * b : 128 * b + 128] = lo
    mid = matmul(row[0], rsplit[0]) + (matmul(row[1], rsplit[0]) + matmul(row[0], rsplit[1]))
    for b in range(3):
        for q in range(2):
            vr = mid[64 * q : 64 * q + 64, 128 * b : 128 * b + 128]
            vi = mid[128 + 64 * q : 192 + 64 * q, 128 * b : 128 * b + 128]
            first = (b * 2 + q) * 64
            for part, value in enumerate((vr * twb[0] + vi * twb[1], vi * twb[0] - vr * twb[1])):
                hi, lo = halves(value)
                vsplit[0, first : first + 64, 128 * part : 128 * part + 128] = hi
                vsplit[1, first : first + 64, 128 * part : 128 * part + 128] = lo
    t_buf[...] = matmul(vsplit[0], last[0]) + (matmul(vsplit[1], last[0]) + matmul(vsplit[0], last[1]))

    k_lane = lax.rem(lax.broadcasted_iota(jnp.int32, (1, 128), 1), 8)
    keep = []
    for b in range(3):
        for q in range(2):
            column = k_lane + 8 * q
            if b == 0:
                keep.append((column >= 16 - w_left).astype(F32))
            elif b == 1:
                keep.append(jnp.ones((1, 128), F32))
            else:
                keep.append((column < w_right).astype(F32))

    def block(n):
        return (t_buf[64 * n : 64 * n + 64, 0:128], t_buf[64 * n : 64 * n + 64, 128:256])

    def group_sum(value, which):
        hi, lo = halves(value)
        return matmul(jnp.concatenate([hi, lo], axis=1), sums[which])

    def normalized(nr, ni):
        both = group_sum(jnp.concatenate([nr, ni], axis=0), 0)
        vr = both[0:64]
        vi = both[64:128]
        power = vr * vr + vi * vi
        mean = jnp.sum(jnp.sum(power, axis=0, keepdims=True), axis=1, keepdims=True) * (1.0 / (8 * N))
        scale = 1.0 / jnp.sqrt(power + mean + EPS)
        return (vr * scale, vi * scale)

    nr = jnp.zeros((64, 128), F32)
    ni = jnp.zeros((64, 128), F32)
    for n in range(6):
        tr, ti = block(n)
        nr = nr + tr * keep[n]
        ni = ni + ti * keep[n]
    ur, ui = normalized(nr, ni)
    for _ in range(ITERS):
        rows = []
        for n in range(6):
            tr, ti = block(n)
            rows.append(jnp.sum(ur * tr + ui * ti, axis=0, keepdims=True) * keep[n])
            rows.append(jnp.sum(ui * tr - ur * ti, axis=0, keepdims=True) * keep[n])
        rows.append(jnp.zeros((4, 128), F32))
        back = group_sum(jnp.concatenate(rows, axis=0), 1)
        nr = jnp.zeros((64, 128), F32)
        ni = jnp.zeros((64, 128), F32)
        for n in range(6):
            tr, ti = block(n)
            br = back[2 * n : 2 * n + 1, :]
            bi = back[2 * n + 1 : 2 * n + 2, :]
            nr = nr + (tr * br - ti * bi)
            ni = ni + (tr * bi + ti * br)
        ur, ui = normalized(nr, ni)

    fixed = [[], []]
    for q in range(2):
        tr, ti = block(2 + q)
        fixed[0].append(ur * tr + ui * ti)
        fixed[1].append(ur * ti - ui * tr)
    left = lax.broadcasted_iota(jnp.int32, (8, 128), 1) < 64
    for part in range(2):
        turned = jnp.concatenate(fixed[part], axis=0).T
        for p in range(8):
            first = turned[16 * p : 16 * p + 8]
            second = turned[16 * p + 8 : 16 * p + 16]
            out_ref[part, 0:8, 128 * p : 128 * p + 128] = jnp.where(left, first, pltpu.roll(second, 64, 1))
            out_ref[part, 8:16, 128 * p : 128 * p + 128] = jnp.where(left, pltpu.roll(first, 64, 1), second)

    for copy in core_copies + y_copies:
        copy.wait_send()
    wait_bytes(r_buf.at[:, pl.ds(0, 31)], a2a_sem.at[0])


def local(reflection, phase, group_index, widths):
    consts = [jnp.asarray(t) for t in tables()]
    operands = [reflection, phase, group_index, widths] + consts
    operands = [pltpu.with_memory_space_constraint(v, pltpu.HBM) for v in operands]
    in_specs = [pl.BlockSpec(memory_space=pltpu.HBM)] * len(operands)
    scratch = [
        pltpu.VMEM((2, NFD, ROWS, N), F32),
        pltpu.VMEM((NFD, N), F32),
        pltpu.SMEM((NFD,), jnp.int32),
        pltpu.SMEM((1, 2), jnp.int32),
        pltpu.VMEM((2, 8, 128), F32),
        pltpu.VMEM((2, 320, 256), BF16),
        pltpu.VMEM((2, 256, 256), BF16),
        pltpu.VMEM((2, 64, 128), F32),
        pltpu.VMEM((2, 256, 256), BF16),
        pltpu.VMEM((2, 256, 128), BF16),
        pltpu.VMEM((2, 2, ROWS, N), F32),
        pltpu.VMEM((2, 2, ROWS, N), F32),
        pltpu.VMEM((2, 2, ROWS, N), F32),
        pltpu.VMEM((2, 2, 128, 256), BF16),
        pltpu.VMEM((2, 2, 160, 128), F32),
        pltpu.VMEM((3, 160, 128), F32),
        pltpu.VMEM((4, 10, 8, 128), F32),
        pltpu.VMEM((3, 32, 8, 128), F32),
        pltpu.VMEM((2, 256, 384), BF16),
        pltpu.VMEM((2, 384, 256), BF16),
        pltpu.VMEM((384, 256), F32),
        pltpu.SemaphoreType.DMA((10,)),
        pltpu.SemaphoreType.DMA((2, 2)),
        pltpu.SemaphoreType.DMA((2, 3 * len(CHUNKS))),
        pltpu.SemaphoreType.DMA((2,)),
        pltpu.SemaphoreType.REGULAR,
    ]
    result = pl.pallas_call(
        kernel,
        out_shape=jax.ShapeDtypeStruct((2, ROWS, N), F32),
        in_specs=in_specs,
        out_specs=pl.BlockSpec(memory_space=pltpu.VMEM),
        scratch_shapes=scratch,
        name="focus",
        compiler_params=pltpu.CompilerParams(
            collective_id=0, has_side_effects=True, vmem_limit_bytes=48 * 1024 * 1024
        ),
    )(*operands)
    return jnp.swapaxes(result, 1, 2)[:, None]


def solution(mesh):
    in_specs = (P(None, "freq", "space", None), P("freq", None), P("freq"), P("space", None))
    out_specs = P(None, "freq", None, "space")
    return jax.shard_map(local, mesh=mesh, in_specs=in_specs, out_specs=out_specs, check_vma=False)
```

```python
import functools
import math

import jax
import jax.numpy as jnp
import ml_dtypes
import numpy as np
from jax import lax
from jax.experimental import pallas as pl
from jax.experimental.pallas import tpu as pltpu
from jax.sharding import PartitionSpec as P

MESH = pl.DeviceIdType.MESH
F32 = jnp.float32
BF16 = jnp.bfloat16
ITERS = 3
N = 1024
NFD = 8
ROWS = 16
EPS = 1e-06
CHUNKS = ((0, 3), (3, 2), (5, 2), (7, 3))


def split_np(table):
    hi = table.astype(np.float32).astype(ml_dtypes.bfloat16)
    lo = (table - hi.astype(np.float64)).astype(np.float32).astype(ml_dtypes.bfloat16)
    return np.stack([hi, lo])


def tables():
    lane = np.arange(128)
    k1 = np.arange(8)
    ang = 2 * np.pi * (k1[:, None] * lane[None, :] % N) / N
    twist_a = np.stack([np.cos(ang), np.sin(ang)]) / 32.0
    k2 = []
    for first, count in CHUNKS:
        y_lo, x, slot, q_hi = np.meshgrid(np.arange(2), np.arange(4), first + np.arange(count), np.arange(2), indexing="ij")
        k2.append((2 * (((x * 2 + y_lo) * 8 + slot - 1) % 64) + q_hi).reshape(-1))
    k2 = np.concatenate(k2)
    ang = 2 * np.pi * (k2[:, None] * lane[None, :] % 128) / 128
    cos, sin = (np.cos(ang), np.sin(ang))
    real_rows = np.concatenate([cos, sin], axis=1)
    imag_rows = np.concatenate([-sin, cos], axis=1)
    col = np.stack([real_rows, imag_rows], axis=1).reshape(320, 256)
    row = np.zeros((2, 2, 2, 64, 4, 8, 2, 2, 2))
    m1 = np.arange(64)
    for mine in range(2):
        for rel in range(2):
            xs, zs = np.meshgrid(np.arange(4), np.arange(8), indexing="ij")
            s = (xs * 2 + (mine ^ rel)) * 8 + zs
            ang = 2 * np.pi * (m1[:, None, None] * s[None] % 64) / 64
            for q in range(2):
                row[mine, 0, q, :, :, :, rel, q, 0] = np.cos(ang)
                row[mine, 0, q, :, :, :, rel, q, 1] = np.sin(ang)
                row[mine, 1, q, :, :, :, rel, q, 0] = -np.sin(ang)
                row[mine, 1, q, :, :, :, rel, q, 1] = np.cos(ang)
    row = row.reshape(2, 256, 256)
    ang = 2 * np.pi * (m1[:, None] * (lane % 16)[None, :] % N) / N
    twist_b = np.stack([np.cos(ang), np.sin(ang)])
    last = np.zeros((2, 8, 16, 2, 16, 8))
    i, m2 = (np.arange(16), np.arange(16))
    ang = 2 * np.pi * (i[:, None] * m2[None, :] % 16) / 16
    for k in range(8):
        last[0, k, :, 0, :, k] = np.cos(ang)
        last[1, k, :, 0, :, k] = np.sin(ang)
        last[0, k, :, 1, :, k] = -np.sin(ang)
        last[1, k, :, 1, :, k] = np.cos(ang)
    last = last.reshape(256, 256) / 32.0
    over_k1 = (lane[:, None] // 8 == lane[None, :] // 8).astype(np.float64)
    over_m2 = (lane[:, None] % 8 == lane[None, :] % 8).astype(np.float64)
    sums = np.stack([np.concatenate([t, t], axis=0) for t in (over_k1, over_m2)]).astype(ml_dtypes.bfloat16)
    return (
        twist_a.astype(np.float32),
        split_np(col),
        np.moveaxis(split_np(row), 0, 1),
        twist_b.astype(np.float32),
        split_np(last),
        sums,
    )


def halves(value):
    hi = value.astype(BF16)
    lo = (value - hi.astype(F32)).astype(BF16)
    return (hi, lo)


def dft4(v):
    (ar, ai), (br, bi), (cr, ci), (dr, di) = v
    pr, pi, mr, mi = (ar + cr, ai + ci, ar - cr, ai - ci)
    qr, qi, nr, ni = (br + dr, bi + di, br - dr, bi - di)
    return [(pr + qr, pi + qi), (mr + ni, mi - nr), (pr - qr, pi - qi), (mr - ni, mi + nr)]


def dft8(v):
    even = dft4(v[0::2])
    odd = dft4(v[1::2])
    half = math.sqrt(0.5)
    o1r, o1i = odd[1]
    o2r, o2i = odd[2]
    o3r, o3i = odd[3]
    turned = [
        odd[0],
        ((o1r + o1i) * half, (o1i - o1r) * half),
        (o2i, -o2r),
        ((o3i - o3r) * half, -(o3r + o3i) * half),
    ]
    low = [(e[0] + t[0], e[1] + t[1]) for e, t in zip(even, turned)]
    high = [(e[0] - t[0], e[1] - t[1]) for e, t in zip(even, turned)]
    return low + high


def matmul(left, right):
    return jnp.dot(left, right, preferred_element_type=F32)


def matmul_t(left, right):
    return lax.dot_general(left, right, (((1,), (1,)), ((), ())), preferred_element_type=F32)


def wait_bytes(ref, sem):
    pltpu.make_async_copy(ref, ref, sem).wait()


def kernel(
    refl_hbm, phase_hbm, group_hbm, widths_hbm, twa_hbm, col_hbm, row_hbm, twb_hbm, last_hbm, sums_hbm,
    out_ref,
    refl, phase, group, widths, twa, col, row, twb, last, sums,
    core_out, core_own, core_in, xsplit, y_out, y_in, q_buf, r_buf, rsplit, vsplit, t_buf,
    load_sem, core_sem, y_sem, a2a_sem, plane_sem,
):
    f = lax.axis_index("freq")
    s = lax.axis_index("space")
    y_hi = f // 2
    core = lax.rem(f, 2)
    x = s // 16
    y_lo = lax.rem(s // 8, 2)
    z = lax.rem(s, 8)

    core_peer = (y_hi * 2 + 1 - core, s)
    other_f = (1 - y_hi) * 2 + core
    other_s = (x * 2 + 1 - y_lo) * 8 + z
    y_peers = [(other_f, s), (f, other_s), (other_f, other_s)]
    own = x * 8 + z

    barrier = pltpu.get_barrier_semaphore()
    z_ring = [(f, (x * 2 + y_lo) * 8 + lax.rem(z + d, 8)) for d in (4, 3, 5, 2, 6, 1, 7)]
    x_ring = [(f, (lax.rem(x + d, 4) * 2 + y_lo) * 8 + z) for d in (2, 1, 3)]
    first_peers = z_ring[:3] + y_peers[:1] + x_ring[:1] + z_ring[3:] + y_peers[1:] + x_ring[1:] + [core_peer]
    for peer in first_peers:
        pl.semaphore_signal(barrier, inc=1, device_id=peer, device_id_type=MESH)

    loads = [
        pltpu.make_async_copy(src, dst, load_sem.at[n])
        for n, (src, dst) in enumerate(
            [
                (group_hbm, group), (phase_hbm, phase), (refl_hbm, refl), (twa_hbm, twa), (col_hbm, col),
                (row_hbm.at[y_lo], row), (twb_hbm, twb), (last_hbm, last), (sums_hbm, sums), (widths_hbm, widths),
            ]
        )
    ]
    for load in loads:
        load.start()

    loads[0].wait()
    loads[1].wait()
    angle = phase[...]
    cosine = jnp.cos(angle)
    sine = jnp.sin(angle)
    weights = [
        [(group[k] == 2 * gh + gc).astype(F32) for gh in range(2) for gc in (1 - core, core)] for k in range(NFD)
    ]
    loads[2].wait()
    def focus(which, target):
        for a in range(8):
            lanes = slice(128 * a, 128 * a + 128)
            total = [[None, None] for _ in range(2)]
            for k in range(NFD):
                c = cosine[k : k + 1, lanes]
                d = sine[k : k + 1, lanes]
                re = refl[0, k, :, lanes]
                im = refl[1, k, :, lanes]
                turned = (re * c - im * d, re * d + im * c)
                for gh in range(2):
                    for part in range(2):
                        term = turned[part] * weights[k][2 * gh + which]
                        total[gh][part] = term if k == 0 else total[gh][part] + term
            for gh in range(2):
                for part in range(2):
                    target[gh, part, :, lanes] = total[gh][part]

    focus(0, core_out)

    pl.semaphore_wait(barrier, len(first_peers))
    groups = (1 - y_hi, y_hi)
    core_copies = [
        pltpu.make_async_remote_copy(
            src_ref=core_out.at[gh], dst_ref=core_in.at[gh], send_sem=core_sem.at[0, n], recv_sem=core_sem.at[1, n],
            device_id=core_peer, device_id_type=MESH,
        )
        for n, gh in enumerate(groups)
    ]
    for copy in core_copies:
        copy.start()
    for peer in x_ring:
        pl.semaphore_signal(plane_sem, inc=1, device_id=peer, device_id_type=MESH)
    focus(1, core_own)
    loads[3].wait()
    loads[4].wait()

    y_copies = []

    def y_part(half, n):
        first, count = CHUNKS[half]
        rows = slice(32 * first, 32 * (first + count))
        y = matmul_t(col[0, rows], xsplit[n, 0]) + (
            matmul_t(col[1, rows], xsplit[n, 0]) + matmul_t(col[0, rows], xsplit[n, 1])
        )
        for index in range(2):
            y_out[n, index, 16 * first : 16 * (first + count)] = y[16 * count * index : 16 * count * (index + 1)]
        for place, peer in ((y_lo, y_peers[0]), (1 - y_lo, y_peers[2])) if n == 0 else ((1 - y_lo, y_peers[1]),):
            slot = len(y_copies)
            part = pl.ds(16 * first, 16 * count)
            copy = pltpu.make_async_remote_copy(
                src_ref=y_out.at[n, place, part], dst_ref=y_in.at[slot % 3, part], send_sem=y_sem.at[0, slot],
                recv_sem=y_sem.at[1, slot], device_id=peer, device_id_type=MESH,
            )
            copy.start()
            y_copies.append(copy)

    for n, gh in enumerate(groups):
        core_copies[n].wait_recv()
        tiles = []
        for a in range(8):
            lanes = slice(128 * a, 128 * a + 128)
            tiles.append(tuple(core_own[gh, part, :, lanes] + core_in[gh, part, :, lanes] for part in range(2)))
        mixed = dft8(tiles)
        for k in range(8):
            vr, vi = mixed[k]
            c = twa[0, k : k + 1, :]
            d = twa[1, k : k + 1, :]
            first = k * ROWS
            for part, value in enumerate((vr * c + vi * d, vi * c - vr * d)):
                hi, lo = halves(value)
                xsplit[n, 0, first : first + ROWS, part * 128 : part * 128 + 128] = hi
                xsplit[n, 1, first : first + ROWS, part * 128 : part * 128 + 128] = lo
        y_part(0, n)
    for half in range(1, len(CHUNKS)):
        for n in range(2):
            y_part(half, n)
    pl.semaphore_wait(plane_sem, 3)

    low = lax.broadcasted_iota(jnp.int32, (8, 128), 0) < 4
    for half, (first, count) in enumerate(CHUNKS):
        for copy in y_copies[3 * half : 3 * half + 3]:
            copy.wait_recv()
        for t in range(2 * count):
            rows = slice(16 * first + 8 * t, 16 * first + 8 * t + 8)
            near = y_out[1, y_lo, rows, :] + y_in[0, rows, :]
            far = y_in[1, rows, :] + y_in[2, rows, :]
            n = 2 * t
            q_buf[n // count, first + n % count] = jnp.where(low, near, pltpu.roll(far, 4, 0))
            n = n + 1
            q_buf[n // count, first + n % count] = jnp.where(low, pltpu.roll(near, 4, 0), far)

        now = [pz for pz in range(8) if first <= pz + 2 < first + count]
        for dx, pz in [(None, pz) for pz in now] + [(dx, pz) for pz in now for dx in (2, 1, 3, 0)]:
            px = 0 if dx is None else lax.rem(x + dx, 4)

            def push(px=px, pz=pz):
                pltpu.make_async_remote_copy(
                    src_ref=q_buf.at[px, pl.ds(pz, 3)], dst_ref=r_buf.at[:, own], send_sem=a2a_sem.at[0],
                    recv_sem=a2a_sem.at[1], device_id=(f, (px * 2 + y_lo) * 8 + pz), device_id_type=MESH,
                ).start()

            other = own != px * 8 + pz
            pl.when(other if dx is None else jnp.logical_and(px != 0, other))(push)
    for b in range(3):
        r_buf[b, own] = q_buf[x, z + b]
    for load in loads[5:]:
        load.wait()
    w_left = widths[0, 0]
    w_right = widths[0, 1]
    wait_bytes(r_buf.at[:, pl.ds(0, 31)], a2a_sem.at[1])

    for b in range(3):
        hi, lo = halves(r_buf[b].reshape(256, 128))
        rsplit[0, :, 128 * b : 128 * b + 128] = hi
        rsplit[1, :, 128 * b : 128 * b + 128] = lo
    mid = matmul(row[0], rsplit[0]) + (matmul(row[1], rsplit[0]) + matmul(row[0], rsplit[1]))
    for b in range(3):
        for q in range(2):
            vr = mid[64 * q : 64 * q + 64, 128 * b : 128 * b + 128]
            vi = mid[128 + 64 * q : 192 + 64 * q, 128 * b : 128 * b + 128]
            first = (b * 2 + q) * 64
            for part, value in enumerate((vr * twb[0] + vi * twb[1], vi * twb[0] - vr * twb[1])):
                hi, lo = halves(value)
                vsplit[0, first : first + 64, 128 * part : 128 * part + 128] = hi
                vsplit[1, first : first + 64, 128 * part : 128 * part + 128] = lo
    t_buf[...] = matmul(vsplit[0], last[0]) + (matmul(vsplit[1], last[0]) + matmul(vsplit[0], last[1]))

    k_lane = lax.rem(lax.broadcasted_iota(jnp.int32, (1, 128), 1), 8)
    keep = []
    for b in range(3):
        for q in range(2):
            column = k_lane + 8 * q
            if b == 0:
                keep.append((column >= 16 - w_left).astype(F32))
            elif b == 1:
                keep.append(jnp.ones((1, 128), F32))
            else:
                keep.append((column < w_right).astype(F32))

    def block(n):
        return (t_buf[64 * n : 64 * n + 64, 0:128], t_buf[64 * n : 64 * n + 64, 128:256])

    def group_sum(value, which):
        hi, lo = halves(value)
        return matmul(jnp.concatenate([hi, lo], axis=1), sums[which])

    def normalized(nr, ni):
        both = group_sum(jnp.concatenate([nr, ni], axis=0), 0)
        vr = both[0:64]
        vi = both[64:128]
        power = vr * vr + vi * vi
        mean = jnp.sum(jnp.sum(power, axis=0, keepdims=True), axis=1, keepdims=True) * (1.0 / (8 * N))
        scale = 1.0 / jnp.sqrt(power + mean + EPS)
        return (vr * scale, vi * scale)

    nr = jnp.zeros((64, 128), F32)
    ni = jnp.zeros((64, 128), F32)
    for n in range(6):
        tr, ti = block(n)
        nr = nr + tr * keep[n]
        ni = ni + ti * keep[n]
    ur, ui = normalized(nr, ni)
    for _ in range(ITERS):
        rows = []
        for n in range(6):
            tr, ti = block(n)
            rows.append(jnp.sum(ur * tr + ui * ti, axis=0, keepdims=True) * keep[n])
            rows.append(jnp.sum(ui * tr - ur * ti, axis=0, keepdims=True) * keep[n])
        rows.append(jnp.zeros((4, 128), F32))
        back = group_sum(jnp.concatenate(rows, axis=0), 1)
        nr = jnp.zeros((64, 128), F32)
        ni = jnp.zeros((64, 128), F32)
        for n in range(6):
            tr, ti = block(n)
            br = back[2 * n : 2 * n + 1, :]
            bi = back[2 * n + 1 : 2 * n + 2, :]
            nr = nr + (tr * br - ti * bi)
            ni = ni + (tr * bi + ti * br)
        ur, ui = normalized(nr, ni)

    fixed = [[], []]
    for q in range(2):
        tr, ti = block(2 + q)
        fixed[0].append(ur * tr + ui * ti)
        fixed[1].append(ur * ti - ui * tr)
    left = lax.broadcasted_iota(jnp.int32, (8, 128), 1) < 64
    for part in range(2):
        turned = jnp.concatenate(fixed[part], axis=0).T
        for p in range(8):
            first = turned[16 * p : 16 * p + 8]
            second = turned[16 * p + 8 : 16 * p + 16]
            out_ref[part, 0:8, 128 * p : 128 * p + 128] = jnp.where(left, first, pltpu.roll(second, 64, 1))
            out_ref[part, 8:16, 128 * p : 128 * p + 128] = jnp.where(left, pltpu.roll(first, 64, 1), second)

    for copy in core_copies + y_copies:
        copy.wait_send()
    wait_bytes(r_buf.at[:, pl.ds(0, 31)], a2a_sem.at[0])


def local(reflection, phase, group_index, widths):
    consts = [jnp.asarray(t) for t in tables()]
    operands = [reflection, phase, group_index, widths] + consts
    operands = [pltpu.with_memory_space_constraint(v, pltpu.HBM) for v in operands]
    in_specs = [pl.BlockSpec(memory_space=pltpu.HBM)] * len(operands)
    scratch = [
        pltpu.VMEM((2, NFD, ROWS, N), F32),
        pltpu.VMEM((NFD, N), F32),
        pltpu.SMEM((NFD,), jnp.int32),
        pltpu.SMEM((1, 2), jnp.int32),
        pltpu.VMEM((2, 8, 128), F32),
        pltpu.VMEM((2, 320, 256), BF16),
        pltpu.VMEM((2, 256, 256), BF16),
        pltpu.VMEM((2, 64, 128), F32),
        pltpu.VMEM((2, 256, 256), BF16),
        pltpu.VMEM((2, 256, 128), BF16),
        pltpu.VMEM((2, 2, ROWS, N), F32),
        pltpu.VMEM((2, 2, ROWS, N), F32),
        pltpu.VMEM((2, 2, ROWS, N), F32),
        pltpu.VMEM((2, 2, 128, 256), BF16),
        pltpu.VMEM((2, 2, 160, 128), F32),
        pltpu.VMEM((3, 160, 128), F32),
        pltpu.VMEM((4, 10, 8, 128), F32),
        pltpu.VMEM((3, 32, 8, 128), F32),
        pltpu.VMEM((2, 256, 384), BF16),
        pltpu.VMEM((2, 384, 256), BF16),
        pltpu.VMEM((384, 256), F32),
        pltpu.SemaphoreType.DMA((10,)),
        pltpu.SemaphoreType.DMA((2, 2)),
        pltpu.SemaphoreType.DMA((2, 3 * len(CHUNKS))),
        pltpu.SemaphoreType.DMA((2,)),
        pltpu.SemaphoreType.REGULAR,
    ]
    result = pl.pallas_call(
        kernel,
        out_shape=jax.ShapeDtypeStruct((2, ROWS, N), F32),
        in_specs=in_specs,
        out_specs=pl.BlockSpec(memory_space=pltpu.VMEM),
        scratch_shapes=scratch,
        name="focus",
        compiler_params=pltpu.CompilerParams(
            collective_id=0, has_side_effects=True, vmem_limit_bytes=48 * 1024 * 1024
        ),
    )(*operands)
    return jnp.swapaxes(result, 1, 2)[:, None]


def solution(mesh):
    in_specs = (P(None, "freq", "space", None), P("freq", None), P("freq"), P("space", None))
    out_specs = P(None, "freq", None, "space")
    return jax.shard_map(local, mesh=mesh, in_specs=in_specs, out_specs=out_specs, check_vma=False)
```

```python
import functools
import math

import jax
import jax.numpy as jnp
import ml_dtypes
import numpy as np
from jax import lax
from jax.experimental import pallas as pl
from jax.experimental.pallas import tpu as pltpu
from jax.sharding import PartitionSpec as P

MESH = pl.DeviceIdType.MESH
F32 = jnp.float32
BF16 = jnp.bfloat16
ITERS = 3
N = 1024
NFD = 8
ROWS = 16
EPS = 1e-06
CHUNKS = ((0, 3), (3, 2), (5, 2), (7, 3))


def split_np(table):
    hi = table.astype(np.float32).astype(ml_dtypes.bfloat16)
    lo = (table - hi.astype(np.float64)).astype(np.float32).astype(ml_dtypes.bfloat16)
    return np.stack([hi, lo])


def tables():
    lane = np.arange(128)
    k1 = np.arange(8)
    ang = 2 * np.pi * (k1[:, None] * lane[None, :] % N) / N
    twist_a = np.stack([np.cos(ang), np.sin(ang)]) / 32.0
    k2 = []
    for first, count in CHUNKS:
        y_lo, x, slot, q_hi = np.meshgrid(np.arange(2), np.arange(4), first + np.arange(count), np.arange(2), indexing="ij")
        k2.append((2 * (((x * 2 + y_lo) * 8 + slot - 1) % 64) + q_hi).reshape(-1))
    k2 = np.concatenate(k2)
    ang = 2 * np.pi * (k2[:, None] * lane[None, :] % 128) / 128
    cos, sin = (np.cos(ang), np.sin(ang))
    real_rows = np.concatenate([cos, sin], axis=1)
    imag_rows = np.concatenate([-sin, cos], axis=1)
    col = np.stack([real_rows, imag_rows], axis=1).reshape(320, 256)
    row = np.zeros((2, 2, 2, 64, 4, 8, 2, 2, 2))
    m1 = np.arange(64)
    for mine in range(2):
        for rel in range(2):
            xs, zs = np.meshgrid(np.arange(4), np.arange(8), indexing="ij")
            s = (xs * 2 + (mine ^ rel)) * 8 + zs
            ang = 2 * np.pi * (m1[:, None, None] * s[None] % 64) / 64
            for q in range(2):
                row[mine, 0, q, :, :, :, rel, q, 0] = np.cos(ang)
                row[mine, 0, q, :, :, :, rel, q, 1] = np.sin(ang)
                row[mine, 1, q, :, :, :, rel, q, 0] = -np.sin(ang)
                row[mine, 1, q, :, :, :, rel, q, 1] = np.cos(ang)
    row = row.reshape(2, 256, 256)
    ang = 2 * np.pi * (m1[:, None] * (lane % 16)[None, :] % N) / N
    twist_b = np.stack([np.cos(ang), np.sin(ang)])
    last = np.zeros((2, 8, 16, 2, 16, 8))
    i, m2 = (np.arange(16), np.arange(16))
    ang = 2 * np.pi * (i[:, None] * m2[None, :] % 16) / 16
    for k in range(8):
        last[0, k, :, 0, :, k] = np.cos(ang)
        last[1, k, :, 0, :, k] = np.sin(ang)
        last[0, k, :, 1, :, k] = -np.sin(ang)
        last[1, k, :, 1, :, k] = np.cos(ang)
    last = last.reshape(256, 256) / 32.0
    over_k1 = (lane[:, None] // 8 == lane[None, :] // 8).astype(np.float64)
    over_m2 = (lane[:, None] % 8 == lane[None, :] % 8).astype(np.float64)
    sums = np.stack([np.concatenate([t, t], axis=0) for t in (over_k1, over_m2)]).astype(ml_dtypes.bfloat16)
    return (
        twist_a.astype(np.float32),
        split_np(col),
        np.moveaxis(split_np(row), 0, 1),
        twist_b.astype(np.float32),
        split_np(last),
        sums,
    )


def halves(value):
    hi = value.astype(BF16)
    lo = (value - hi.astype(F32)).astype(BF16)
    return (hi, lo)


def dft4(v):
    (ar, ai), (br, bi), (cr, ci), (dr, di) = v
    pr, pi, mr, mi = (ar + cr, ai + ci, ar - cr, ai - ci)
    qr, qi, nr, ni = (br + dr, bi + di, br - dr, bi - di)
    return [(pr + qr, pi + qi), (mr + ni, mi - nr), (pr - qr, pi - qi), (mr - ni, mi + nr)]


def dft8(v):
    even = dft4(v[0::2])
    odd = dft4(v[1::2])
    half = math.sqrt(0.5)
    o1r, o1i = odd[1]
    o2r, o2i = odd[2]
    o3r, o3i = odd[3]
    turned = [
        odd[0],
        ((o1r + o1i) * half, (o1i - o1r) * half),
        (o2i, -o2r),
        ((o3i - o3r) * half, -(o3r + o3i) * half),
    ]
    low = [(e[0] + t[0], e[1] + t[1]) for e, t in zip(even, turned)]
    high = [(e[0] - t[0], e[1] - t[1]) for e, t in zip(even, turned)]
    return low + high


def matmul(left, right):
    return jnp.dot(left, right, preferred_element_type=F32)


def matmul_t(left, right):
    return lax.dot_general(left, right, (((1,), (1,)), ((), ())), preferred_element_type=F32)


def wait_bytes(ref, sem):
    pltpu.make_async_copy(ref, ref, sem).wait()


def kernel(
    refl_hbm, phase_hbm, group_hbm, widths_hbm, twa_hbm, col_hbm, row_hbm, twb_hbm, last_hbm, sums_hbm,
    out_ref,
    refl, phase, group, widths, twa, col, row, twb, last, sums,
    core_out, core_own, core_in, xsplit, y_out, y_in, q_buf, r_buf, rsplit, vsplit, t_buf,
    load_sem, core_sem, y_sem, a2a_sem, plane_sem,
):
    f = lax.axis_index("freq")
    s = lax.axis_index("space")
    y_hi = f // 2
    core = lax.rem(f, 2)
    x = s // 16
    y_lo = lax.rem(s // 8, 2)
    z = lax.rem(s, 8)

    core_peer = (y_hi * 2 + 1 - core, s)
    other_f = (1 - y_hi) * 2 + core
    other_s = (x * 2 + 1 - y_lo) * 8 + z
    y_peers = [(other_f, s), (f, other_s), (other_f, other_s)]
    own = x * 8 + z

    barrier = pltpu.get_barrier_semaphore()
    z_ring = [(f, (x * 2 + y_lo) * 8 + lax.rem(z + d, 8)) for d in (4, 3, 5, 2, 6, 1, 7)]
    x_ring = [(f, (lax.rem(x + d, 4) * 2 + y_lo) * 8 + z) for d in (2, 1, 3)]
    first_peers = z_ring[:3] + y_peers[:1] + x_ring[:1] + z_ring[3:] + y_peers[1:] + x_ring[1:] + [core_peer]
    for peer in first_peers:
        pl.semaphore_signal(barrier, inc=1, device_id=peer, device_id_type=MESH)

    loads = [
        pltpu.make_async_copy(src, dst, load_sem.at[n])
        for n, (src, dst) in enumerate(
            [
                (group_hbm, group), (phase_hbm, phase), (refl_hbm, refl), (twa_hbm, twa), (col_hbm, col),
                (row_hbm.at[y_lo], row), (twb_hbm, twb), (last_hbm, last), (sums_hbm, sums), (widths_hbm, widths),
            ]
        )
    ]
    for load in loads[:3]:
        load.start()

    loads[0].wait()
    loads[1].wait()
    angle = phase[...]
    cosine = jnp.cos(angle)
    sine = jnp.sin(angle)
    weights = [
        [(group[k] == 2 * gh + gc).astype(F32) for gh in range(2) for gc in (1 - core, core)] for k in range(NFD)
    ]
    loads[2].wait()
    for load in loads[3:]:
        load.start()
    def focus(which, target):
        for a in range(8):
            lanes = slice(128 * a, 128 * a + 128)
            total = [[None, None] for _ in range(2)]
            for k in range(NFD):
                c = cosine[k : k + 1, lanes]
                d = sine[k : k + 1, lanes]
                re = refl[0, k, :, lanes]
                im = refl[1, k, :, lanes]
                turned = (re * c - im * d, re * d + im * c)
                for gh in range(2):
                    for part in range(2):
                        term = turned[part] * weights[k][2 * gh + which]
                        total[gh][part] = term if k == 0 else total[gh][part] + term
            for gh in range(2):
                for part in range(2):
                    target[gh, part, :, lanes] = total[gh][part]

    focus(0, core_out)

    pl.semaphore_wait(barrier, len(first_peers))
    groups = (1 - y_hi, y_hi)
    core_copies = [
        pltpu.make_async_remote_copy(
            src_ref=core_out.at[gh], dst_ref=core_in.at[gh], send_sem=core_sem.at[0, n], recv_sem=core_sem.at[1, n],
            device_id=core_peer, device_id_type=MESH,
        )
        for n, gh in enumerate(groups)
    ]
    for copy in core_copies:
        copy.start()
    for peer in x_ring:
        pl.semaphore_signal(plane_sem, inc=1, device_id=peer, device_id_type=MESH)
    focus(1, core_own)
    loads[3].wait()
    loads[4].wait()

    y_copies = []

    def y_part(half, n):
        first, count = CHUNKS[half]
        rows = slice(32 * first, 32 * (first + count))
        y = matmul_t(col[0, rows], xsplit[n, 0]) + (
            matmul_t(col[1, rows], xsplit[n, 0]) + matmul_t(col[0, rows], xsplit[n, 1])
        )
        for index in range(2):
            y_out[n, index, 16 * first : 16 * (first + count)] = y[16 * count * index : 16 * count * (index + 1)]
        for place, peer in ((y_lo, y_peers[0]), (1 - y_lo, y_peers[2])) if n == 0 else ((1 - y_lo, y_peers[1]),):
            slot = len(y_copies)
            part = pl.ds(16 * first, 16 * count)
            copy = pltpu.make_async_remote_copy(
                src_ref=y_out.at[n, place, part], dst_ref=y_in.at[slot % 3, part], send_sem=y_sem.at[0, slot],
                recv_sem=y_sem.at[1, slot], device_id=peer, device_id_type=MESH,
            )
            copy.start()
            y_copies.append(copy)

    for n, gh in enumerate(groups):
        core_copies[n].wait_recv()
        tiles = []
        for a in range(8):
            lanes = slice(128 * a, 128 * a + 128)
            tiles.append(tuple(core_own[gh, part, :, lanes] + core_in[gh, part, :, lanes] for part in range(2)))
        mixed = dft8(tiles)
        for k in range(8):
            vr, vi = mixed[k]
            c = twa[0, k : k + 1, :]
            d = twa[1, k : k + 1, :]
            first = k * ROWS
            for part, value in enumerate((vr * c + vi * d, vi * c - vr * d)):
                hi, lo = halves(value)
                xsplit[n, 0, first : first + ROWS, part * 128 : part * 128 + 128] = hi
                xsplit[n, 1, first : first + ROWS, part * 128 : part * 128 + 128] = lo
        y_part(0, n)
    for half in range(1, len(CHUNKS)):
        for n in range(2):
            y_part(half, n)
    pl.semaphore_wait(plane_sem, 3)

    low = lax.broadcasted_iota(jnp.int32, (8, 128), 0) < 4
    for half, (first, count) in enumerate(CHUNKS):
        for copy in y_copies[3 * half : 3 * half + 3]:
            copy.wait_recv()
        for t in range(2 * count):
            rows = slice(16 * first + 8 * t, 16 * first + 8 * t + 8)
            near = y_out[1, y_lo, rows, :] + y_in[0, rows, :]
            far = y_in[1, rows, :] + y_in[2, rows, :]
            n = 2 * t
            q_buf[n // count, first + n % count] = jnp.where(low, near, pltpu.roll(far, 4, 0))
            n = n + 1
            q_buf[n // count, first + n % count] = jnp.where(low, pltpu.roll(near, 4, 0), far)

        now = [pz for pz in range(8) if first <= pz + 2 < first + count]
        for dx, pz in [(None, pz) for pz in now] + [(dx, pz) for pz in now for dx in (2, 1, 3, 0)]:
            px = 0 if dx is None else lax.rem(x + dx, 4)

            def push(px=px, pz=pz):
                pltpu.make_async_remote_copy(
                    src_ref=q_buf.at[px, pl.ds(pz, 3)], dst_ref=r_buf.at[:, own], send_sem=a2a_sem.at[0],
                    recv_sem=a2a_sem.at[1], device_id=(f, (px * 2 + y_lo) * 8 + pz), device_id_type=MESH,
                ).start()

            other = own != px * 8 + pz
            pl.when(other if dx is None else jnp.logical_and(px != 0, other))(push)
    for b in range(3):
        r_buf[b, own] = q_buf[x, z + b]
    for load in loads[5:]:
        load.wait()
    w_left = widths[0, 0]
    w_right = widths[0, 1]
    wait_bytes(r_buf.at[:, pl.ds(0, 31)], a2a_sem.at[1])

    for b in range(3):
        hi, lo = halves(r_buf[b].reshape(256, 128))
        rsplit[0, :, 128 * b : 128 * b + 128] = hi
        rsplit[1, :, 128 * b : 128 * b + 128] = lo
    mid = matmul(row[0], rsplit[0]) + (matmul(row[1], rsplit[0]) + matmul(row[0], rsplit[1]))
    for b in range(3):
        for q in range(2):
            vr = mid[64 * q : 64 * q + 64, 128 * b : 128 * b + 128]
            vi = mid[128 + 64 * q : 192 + 64 * q, 128 * b : 128 * b + 128]
            first = (b * 2 + q) * 64
            for part, value in enumerate((vr * twb[0] + vi * twb[1], vi * twb[0] - vr * twb[1])):
                hi, lo = halves(value)
                vsplit[0, first : first + 64, 128 * part : 128 * part + 128] = hi
                vsplit[1, first : first + 64, 128 * part : 128 * part + 128] = lo
    t_buf[...] = matmul(vsplit[0], last[0]) + (matmul(vsplit[1], last[0]) + matmul(vsplit[0], last[1]))

    k_lane = lax.rem(lax.broadcasted_iota(jnp.int32, (1, 128), 1), 8)
    keep = []
    for b in range(3):
        for q in range(2):
            column = k_lane + 8 * q
            if b == 0:
                keep.append((column >= 16 - w_left).astype(F32))
            elif b == 1:
                keep.append(jnp.ones((1, 128), F32))
            else:
                keep.append((column < w_right).astype(F32))

    def block(n):
        return (t_buf[64 * n : 64 * n + 64, 0:128], t_buf[64 * n : 64 * n + 64, 128:256])

    def group_sum(value, which):
        hi, lo = halves(value)
        return matmul(jnp.concatenate([hi, lo], axis=1), sums[which])

    def normalized(nr, ni):
        both = group_sum(jnp.concatenate([nr, ni], axis=0), 0)
        vr = both[0:64]
        vi = both[64:128]
        power = vr * vr + vi * vi
        mean = jnp.sum(jnp.sum(power, axis=0, keepdims=True), axis=1, keepdims=True) * (1.0 / (8 * N))
        scale = 1.0 / jnp.sqrt(power + mean + EPS)
        return (vr * scale, vi * scale)

    nr = jnp.zeros((64, 128), F32)
    ni = jnp.zeros((64, 128), F32)
    for n in range(6):
        tr, ti = block(n)
        nr = nr + tr * keep[n]
        ni = ni + ti * keep[n]
    ur, ui = normalized(nr, ni)
    for _ in range(ITERS):
        rows = []
        for n in range(6):
            tr, ti = block(n)
            rows.append(jnp.sum(ur * tr + ui * ti, axis=0, keepdims=True) * keep[n])
            rows.append(jnp.sum(ui * tr - ur * ti, axis=0, keepdims=True) * keep[n])
        rows.append(jnp.zeros((4, 128), F32))
        back = group_sum(jnp.concatenate(rows, axis=0), 1)
        nr = jnp.zeros((64, 128), F32)
        ni = jnp.zeros((64, 128), F32)
        for n in range(6):
            tr, ti = block(n)
            br = back[2 * n : 2 * n + 1, :]
            bi = back[2 * n + 1 : 2 * n + 2, :]
            nr = nr + (tr * br - ti * bi)
            ni = ni + (tr * bi + ti * br)
        ur, ui = normalized(nr, ni)

    fixed = [[], []]
    for q in range(2):
        tr, ti = block(2 + q)
        fixed[0].append(ur * tr + ui * ti)
        fixed[1].append(ur * ti - ui * tr)
    left = lax.broadcasted_iota(jnp.int32, (8, 128), 1) < 64
    for part in range(2):
        turned = jnp.concatenate(fixed[part], axis=0).T
        for p in range(8):
            first = turned[16 * p : 16 * p + 8]
            second = turned[16 * p + 8 : 16 * p + 16]
            out_ref[part, 0:8, 128 * p : 128 * p + 128] = jnp.where(left, first, pltpu.roll(second, 64, 1))
            out_ref[part, 8:16, 128 * p : 128 * p + 128] = jnp.where(left, pltpu.roll(first, 64, 1), second)

    for copy in core_copies + y_copies:
        copy.wait_send()
    wait_bytes(r_buf.at[:, pl.ds(0, 31)], a2a_sem.at[0])


def local(reflection, phase, group_index, widths):
    consts = [jnp.asarray(t) for t in tables()]
    operands = [reflection, phase, group_index, widths] + consts
    operands = [pltpu.with_memory_space_constraint(v, pltpu.HBM) for v in operands]
    in_specs = [pl.BlockSpec(memory_space=pltpu.HBM)] * len(operands)
    scratch = [
        pltpu.VMEM((2, NFD, ROWS, N), F32),
        pltpu.VMEM((NFD, N), F32),
        pltpu.SMEM((NFD,), jnp.int32),
        pltpu.SMEM((1, 2), jnp.int32),
        pltpu.VMEM((2, 8, 128), F32),
        pltpu.VMEM((2, 320, 256), BF16),
        pltpu.VMEM((2, 256, 256), BF16),
        pltpu.VMEM((2, 64, 128), F32),
        pltpu.VMEM((2, 256, 256), BF16),
        pltpu.VMEM((2, 256, 128), BF16),
        pltpu.VMEM((2, 2, ROWS, N), F32),
        pltpu.VMEM((2, 2, ROWS, N), F32),
        pltpu.VMEM((2, 2, ROWS, N), F32),
        pltpu.VMEM((2, 2, 128, 256), BF16),
        pltpu.VMEM((2, 2, 160, 128), F32),
        pltpu.VMEM((3, 160, 128), F32),
        pltpu.VMEM((4, 10, 8, 128), F32),
        pltpu.VMEM((3, 32, 8, 128), F32),
        pltpu.VMEM((2, 256, 384), BF16),
        pltpu.VMEM((2, 384, 256), BF16),
        pltpu.VMEM((384, 256), F32),
        pltpu.SemaphoreType.DMA((10,)),
        pltpu.SemaphoreType.DMA((2, 2)),
        pltpu.SemaphoreType.DMA((2, 3 * len(CHUNKS))),
        pltpu.SemaphoreType.DMA((2,)),
        pltpu.SemaphoreType.REGULAR,
    ]
    result = pl.pallas_call(
        kernel,
        out_shape=jax.ShapeDtypeStruct((2, ROWS, N), F32),
        in_specs=in_specs,
        out_specs=pl.BlockSpec(memory_space=pltpu.VMEM),
        scratch_shapes=scratch,
        name="focus",
        compiler_params=pltpu.CompilerParams(
            collective_id=0, has_side_effects=True, vmem_limit_bytes=48 * 1024 * 1024
        ),
    )(*operands)
    return jnp.swapaxes(result, 1, 2)[:, None]


def solution(mesh):
    in_specs = (P(None, "freq", "space", None), P("freq", None), P("freq"), P("space", None))
    out_specs = P(None, "freq", None, "space")
    return jax.shard_map(local, mesh=mesh, in_specs=in_specs, out_specs=out_specs, check_vma=False)
```
